32 devices in a mesh: groups: 2 (over y), pool: 8 (over z, x), heads: 2 (over core).
Axes of the slice: x: 2, y: 2, z: 4, core: 2. Of those that a mesh axis runs over, the one named last changes fastest.
Arguments:
- q_latent: bfloat16 [128, 65536], P(('groups', 'pool'), 'heads'), parts along dimension 0, may hold values from -100 to 100
- q_rope: bfloat16 [128, 8192], P(('groups', 'pool'), 'heads'), parts along dimension 0, may hold values from -6 to 6
- cache_latent: bfloat16 [32768, 512], P(('groups', 'pool')), parts along dimension 0, may hold values from -4 to 4
- cache_rope: bfloat16 [64, 32768], P(None, ('groups', 'pool')), parts along dimension 1, may hold values from -6 to 6
- lengths: int32 [16, 8], P(('groups', 'pool')), parts along dimension 0, may hold values from 1 to 1024, 2048 in all within a row
- tokens_b: bfloat16 [32, 3584], P(('groups', 'pool')), parts along dimension 0, may hold values from -6 to 6
- routes: int32 [32, 8], P(('groups', 'pool')), parts along dimension 0, may hold values from 0 to 15, all different within a row; in each aligned block of 2 rows (0 to 1, 2 to 3, ...) at most 2 rows name the same one
- gates: bfloat16 [32, 8], P(('groups', 'pool')), parts along dimension 0, may hold values from 0.049804688 to 0.5
- w_gate: bfloat16 [3584, 32768], P(None, ('pool', 'heads')), may hold values from -0.09375 to 0.09375
- w_up: bfloat16 [3584, 32768], P(None, ('pool', 'heads')), may hold values from -0.09375 to 0.09375
- w_down: bfloat16 [32768, 3584], P(('pool', 'heads')), may hold values from -0.125 to 0.125
Outputs:
- attended: bfloat16 [128, 65536], P(('groups', 'pool'), 'heads'), parts along dimension 0
- moe_out: bfloat16 [32, 3584], P(('groups', 'pool')), parts along dimension 0
The draws below stay inside these ranges and needn't reach their ends.
There are 2 independent parts, one for each index of `groups`. The reference program is written for one: setup_inputs(seed, part) draws one part's arguments, and reference() takes and returns one part's arrays. A program takes and returns all parts, laid end to end along the dimension named above; an argument that names none is the same for every part. Nothing has to cross between parts.
Inputs may be any that keep to these rules, and one draw needn't show every extreme that they name: In each row the lengths sum to 2048 and the largest equals 1024 exactly. `routes`: each row names 8 different experts. Among the 2 rows of one pool device no expert is named by more than 2 rows, and in some pool device's rows one expert is named by exactly 2 rows.
All inputs are finite; a program needn't handle non-finite values.
Results may differ from the reference program's by a relative error of at most 0.005.
Values may be sent and summed in bfloat16 or wider, within the bound.
No kernel may reach another device: no remote copies, remote signals or barrier semaphores. Data moves between devices by JAX's collectives and lax.ppermute only.
A program may use at most 128 MiB of HBM per device.

```python
import math
import jax
import jax.numpy as jnp
import numpy as np
from jax import lax

D = 3584
HEADS = 128
LAT = 512
ROPE = 64
FF = 2048
EXPERTS = 16
TOP = 8
REQ_DEV = 8
CACHE_DEV = 2048
TOK_DEV = 2
CAP = 2
POOLS = 8
REQS = 64
TOTAL = 16384
TOKENS = 16


def shared_keys(key):
    table = jax.random.normal(jax.random.fold_in(key, 101), (TOTAL, LAT), jnp.float32)
    return jnp.clip(table, -4.0, 4.0)


def draw_cache_latent(key, part):
    key_table = shared_keys(key)
    return key_table.astype(jnp.bfloat16)


def draw_q_latent(key, part):
    key = jax.random.fold_in(key, 5)
    block_shape = (POOLS, REQ_DEV, HEADS, LAT)
    jitter = jax.random.normal(key, block_shape, jnp.float32)
    return jnp.clip(jitter, -100.0, 100.0).reshape(REQS, HEADS * LAT).astype(jnp.bfloat16)


def level_of(own_key, dims, split, smallest, largest):
    factor_of, own = 1.0, jax.random.fold_in(own_key, 6)
    for dim, shards_of in split:
        draws = jnp.exp(jax.random.uniform(jax.random.fold_in(own, dim), (shards_of,), jnp.float32, smallest / len(split), largest / len(split)))
        factor_of = factor_of * jnp.repeat(draws, dims[dim] // shards_of).reshape([-1 if axis == dim else 1 for axis in range(len(dims))])
    return factor_of


def split_up(number_of, total, bound, slope):
    weights = [(1 << 20) // math.isqrt(grade ** slope) + 1 for grade in range(2, number_of + 1)]
    rest, counts = total - bound - (number_of - 1), [1] * (number_of - 1)
    while rest > 0:
        free = [i for i in range(number_of - 1) if counts[i] < bound]
        pool, remaining = sum([weights[i] for i in free]), rest
        for i in free:
            addition = min(bound - counts[i], max(1, remaining * weights[i] // pool), rest)
            counts[i] = counts[i] + addition
            rest = rest - addition
    return np.array([bound] + counts)


def ragged(key, count, total, limit, lean):
    if count == 2:
        one = jax.random.randint(key, (), max(1, total - limit), min(limit, total - 1) + 1)
        return jnp.stack([one, total - one])
    tallies = jnp.asarray(split_up(count, total, limit, lean), jnp.int32)
    pairs = (count - 1) // 2
    giver, taker = tallies[1:1 + 2 * pairs:2], tallies[2:2 + 2 * pairs:2]
    margin = jnp.minimum(giver - 1, limit - taker)
    shifted = jax.random.randint(jax.random.fold_in(key, 1), (pairs,), 0, 1 << 20) % (margin + 1)
    tallies = tallies.at[1:1 + 2 * pairs:2].set(giver - shifted).at[2:2 + 2 * pairs:2].set(taker + shifted)
    return tallies[jax.random.permutation(jax.random.fold_in(key, 2), count)]


def routed_block(key, own, number, rows, number_of, top, most, skew):
    order = jax.random.permutation(key, number_of)
    crowded, common = portions_of(number_of, rows * top, most, skew, True), portions_of(number_of, rows * top, most, skew, False)
    places = jnp.arange(number_of)

    def named(tallies, offset_by):
        used = int((tallies > 0).sum())
        fixed = max(1, used // 4)
        passed = fixed + (places - fixed + offset_by * (used - fixed)) % max(1, number_of - fixed)
        return jnp.zeros((number_of,), jnp.int32).at[order[jnp.where(places < fixed, places, passed)]].set(jnp.asarray(tallies, jnp.int32))

    tallies = jnp.where(number % 4 == 0, named(crowded, number // 4), named(common, number - number // 4 - 1))
    mixed = jax.random.permutation(jax.random.fold_in(own, 3), number_of)
    donor, receiver = mixed[0:number_of // 2 * 2:2], mixed[1:number_of // 2 * 2:2]
    room = jnp.minimum(tallies[donor] - 1, most - tallies[receiver]) // 2
    room = jnp.where((donor == order[0]) | (receiver == order[0]) | (tallies[receiver] == 0), 0, jnp.maximum(room, 0))
    passed = jax.random.randint(jax.random.fold_in(own, 4), (number_of // 2,), 0, 1 << 20) % (room + 1)
    tallies = tallies.at[donor].add(-passed).at[receiver].add(passed)
    items = jnp.searchsorted(jnp.cumsum(tallies), jnp.arange(rows * top), side="right").astype(jnp.int32)
    listing = items.reshape(top, rows).T
    listing = listing[jax.random.permutation(jax.random.fold_in(own, 1), rows)]
    offset_by = jax.random.randint(jax.random.fold_in(own, 2), (rows, 1), 0, top)
    return jnp.take_along_axis(listing, (jnp.arange(top)[None, :] + offset_by) % top, axis=1)


def portions_of(count, total, limit, lean, full):
    weights = [(1 << 20) // math.isqrt(rank ** lean) + 1 for rank in range(1, count + 1)]
    largest = limit if full else min(limit, max(-(-total // count), total * weights[0] // sum(weights)))
    least = 1 if total - largest >= count - 1 else 0
    holding, rest = [largest] + [least] * (count - 1), total - largest - least * (count - 1)
    while rest > 0:
        movable = [i for i in range(1, count) if holding[i] < largest] or [i for i in range(1, count) if holding[i] < limit]
        pool, budget = sum([weights[i] for i in movable]), rest
        for i in movable:
            addition = min(limit - holding[i], max(1, budget * weights[i] // pool), rest)
            holding[i] = holding[i] + addition
            rest = rest - addition
    return np.array(holding)


def centred(stream_key, extent, width, most, split=(), kind=jnp.bfloat16):
    entries = width * jax.random.normal(stream_key, extent, jnp.float32)
    if split:
        entries = entries * level_of(stream_key, extent, split, -0.22, 0.18)
    return jnp.clip(entries, -most, most).astype(kind)


def setup_inputs(seed: int = 0, part: int = 0) -> dict:
    key_of = jax.random.split(jax.random.key(seed), 12)
    part_keys = jax.random.split(jax.random.fold_in(key_of[11], part), 12)
    q_latent = draw_q_latent(jax.random.fold_in(jax.random.fold_in(key_of[11], part), 71), part)
    q_rope = centred(part_keys[1], (REQS, HEADS * ROPE), 1.0, 6.0, ((0, 8), (1, 2)))
    cache_latent = draw_cache_latent(jax.random.fold_in(jax.random.fold_in(key_of[11], part), 71), part)
    cache_rope = centred(part_keys[3], (ROPE, TOTAL), 1.0, 6.0, ((1, 8),))
    lengths = jax.vmap(lambda own: ragged(own, REQ_DEV, CACHE_DEV, CACHE_DEV // 2, 2))(jax.random.split(part_keys[4], POOLS)).reshape((POOLS, REQ_DEV)).astype(jnp.int32)
    tokens_b = centred(part_keys[5], (TOKENS, D), 1.0, 6.0, ((0, 8),))
    routes_keys = jax.random.split(jax.random.fold_in(part_keys[6], 1), TOKENS // TOK_DEV)
    routes_turns = jax.random.permutation(jax.random.fold_in(part_keys[6], 3), TOKENS // TOK_DEV)
    routes = jax.vmap(lambda own, number: routed_block(jax.random.fold_in(part_keys[6], 2), own, number, TOK_DEV, EXPERTS, TOP, CAP, 2))(routes_keys, routes_turns).reshape((TOKENS, TOP))
    gates = jnp.clip(jnp.exp(math.log(0.5) - 2.306499 * jax.random.uniform(part_keys[7], (TOKENS, TOP), jnp.float32) ** level_of(part_keys[7], (TOKENS, TOP), ((0, 8),), -0.2, 0.2)), 0.049804688, 0.5).astype(jnp.bfloat16)
    w_gate = centred(key_of[8], (D, EXPERTS * FF), D ** -0.5, 0.09375, ((1, 16),))
    w_up = centred(key_of[9], (D, EXPERTS * FF), D ** -0.5, 0.09375, ((1, 16),))
    w_down = centred(key_of[10], (EXPERTS * FF, D), FF ** -0.5, 0.125, ((0, 16),))
    return {"q_latent": q_latent, "q_rope": q_rope, "cache_latent": cache_latent, "cache_rope": cache_rope, "lengths": lengths, "tokens_b": tokens_b, "routes": routes, "gates": gates, "w_gate": w_gate, "w_up": w_up, "w_down": w_down}


score_scale = 192.0 ** -0.5


def attend(queries, rope_queries, latent, rope_keys, request_lengths):
    requests = request_lengths.shape[0]
    heads_here = queries.shape[0] // requests
    scores = lax.dot_general(queries, latent, (((1,), (1,)), ((), ())), preferred_element_type=jnp.float32)
    scores = (scores + jnp.dot(rope_queries, rope_keys, preferred_element_type=jnp.float32)) * score_scale
    finish = jnp.cumsum(request_lengths).astype(jnp.int32)
    starts = (finish - request_lengths).astype(jnp.int32)
    position = jnp.arange(latent.shape[0], dtype=jnp.int32)
    inside = (position[None, :] >= starts[:, None]) & (position[None, :] < finish[:, None])
    inside = jnp.repeat(inside, heads_here, axis=0)
    scores = jnp.where(inside, scores, -jnp.inf)
    highest = jnp.max(scores, axis=1, keepdims=True)
    weights = jnp.exp(scores - highest)
    shares = (weights / jnp.sum(weights, axis=1, keepdims=True)).astype(jnp.bfloat16)
    return jnp.dot(shares, latent, preferred_element_type=jnp.float32).astype(jnp.bfloat16)


def expert_weights(routes, gates):
    labels = jnp.arange(EXPERTS, dtype=jnp.int32)
    chosen = (routes[:, :, None] == labels[None, None, :]).astype(jnp.float32)
    return jnp.sum(gates.astype(jnp.float32)[:, :, None] * chosen, axis=1)


def expert_block(token_rows, gate_cols, up_cols, down_rows):
    gate_pre = jnp.dot(token_rows, gate_cols, preferred_element_type=jnp.float32)
    up_pre = jnp.dot(token_rows, up_cols, preferred_element_type=jnp.float32)
    hidden = (jax.nn.silu(gate_pre) * up_pre).astype(jnp.bfloat16)
    return jnp.dot(hidden, down_rows, preferred_element_type=jnp.float32)


def reference(q_latent, q_rope, cache_latent, cache_rope, lengths, tokens_b, routes, gates, w_gate, w_up, w_down):
    query_blocks = q_latent.reshape(POOLS, REQ_DEV * HEADS, LAT)
    rope_blocks = q_rope.reshape(POOLS, REQ_DEV * HEADS, ROPE)
    latent_blocks = cache_latent.reshape(POOLS, CACHE_DEV, LAT)
    key_blocks = cache_rope.reshape(ROPE, POOLS, CACHE_DEV).transpose(1, 0, 2)

    def attend_block(block_items):
        return attend(block_items[0], block_items[1], block_items[2], block_items[3], block_items[4])

    attended = lax.map(attend_block, (query_blocks, rope_blocks, latent_blocks, key_blocks, lengths))
    attended = attended.reshape(REQS, HEADS * LAT)

    gate_table = expert_weights(routes, gates)

    def one_expert(running, expert_id):
        first_col = expert_id * FF
        gate_cols = lax.dynamic_slice_in_dim(w_gate, first_col, FF, 1)
        up_cols = lax.dynamic_slice_in_dim(w_up, first_col, FF, 1)
        down_rows = lax.dynamic_slice_in_dim(w_down, first_col, FF, 0)
        column = lax.dynamic_slice_in_dim(gate_table, expert_id, 1, 1)
        return running + expert_block(tokens_b, gate_cols, up_cols, down_rows) * column, None

    start_sum = jnp.zeros((TOKENS, D), jnp.float32)
    total_sum, unused = lax.scan(one_expert, start_sum, jnp.arange(EXPERTS, dtype=jnp.int32))
    return attended, total_sum.astype(jnp.bfloat16)
```

```python
import functools

import jax
import jax.numpy as jnp
from jax import lax
from jax.experimental import pallas as pl
from jax.experimental.pallas import tpu as pltpu
from jax.sharding import PartitionSpec as P

EXPERTS = 16
LANES = 128

score_scale = 192.0 ** (-0.5)


def attend(queries, rope_queries, latent, rope_keys, request_lengths):
    requests = request_lengths.shape[0]
    heads_here = queries.shape[0] // requests
    scores = lax.dot_general(
        queries, latent, (((1,), (1,)), ((), ())), preferred_element_type=jnp.float32
    )
    scores = (
        scores + jnp.dot(rope_queries, rope_keys, preferred_element_type=jnp.float32)
    ) * score_scale
    finish = jnp.cumsum(request_lengths)
    starts = finish - request_lengths
    position = jnp.arange(latent.shape[0], dtype=jnp.int32)
    inside = (position[None, :] >= starts[:, None]) & (position[None, :] < finish[:, None])
    inside = jnp.repeat(inside, heads_here, axis=0)
    scores = jnp.where(inside, scores, -jnp.inf)
    highest = jnp.max(scores, axis=1, keepdims=True)
    weights = jnp.exp(scores - highest)
    shares = (weights / jnp.sum(weights, axis=1, keepdims=True)).astype(jnp.bfloat16)
    return jnp.dot(shares, latent, preferred_element_type=jnp.float32).astype(jnp.bfloat16)


def expert_weights(routes, gates):
    labels = jnp.arange(LANES, dtype=jnp.int32)
    chosen = (routes[:, :, None] == labels[None, None, :]).astype(jnp.float32)
    return jnp.sum(gates.astype(jnp.float32)[:, :, None] * chosen, axis=1)


def row_step(total, most=512):
    return next(s for s in (512, 256, 128, 64, 32, 16) if s <= most and total % s == 0)


def cuts(array):
    step = row_step(array.shape[0])
    return [(k, step) for k in range(0, array.shape[0], step)]


def expert_kernel(own_ref, rows_ref, gate_ref, up_ref, down_ref, out_ref, gate_buf, up_buf, down_buf, sems):
    width = down_ref.shape[1]
    ff = gate_ref.shape[1]
    count = rows_ref.shape[0] * rows_ref.shape[1]
    copies, pending = {}, 0
    for name, source, target in (("gate", gate_ref, gate_buf), ("up", up_ref, up_buf), ("down", down_ref, down_buf)):
        copies[name] = []
        for k, step in cuts(source):
            rows = pl.ds(k, step)
            copies[name].append(pltpu.make_async_copy(source.at[rows], target.at[rows], sems.at[pending]))
            copies[name][-1].start()
            pending += 1
    packed = rows_ref[...].reshape(count, rows_ref.shape[2])
    gate_pre = jnp.zeros((count, ff), jnp.float32)
    up_pre = jnp.zeros((count, ff), jnp.float32)
    for (k, step), copy in zip(cuts(gate_ref), copies["gate"]):
        copy.wait()
        gate_pre += jnp.dot(
            packed[:, k : k + step], gate_buf[k : k + step, :], preferred_element_type=jnp.float32
        )
    for (k, step), copy in zip(cuts(up_ref), copies["up"]):
        copy.wait()
        up_pre += jnp.dot(
            packed[:, k : k + step], up_buf[k : k + step, :], preferred_element_type=jnp.float32
        )
    hidden = (gate_pre / (1.0 + jnp.exp(-gate_pre)) * up_pre).astype(jnp.bfloat16)
    table = packed[:, width:].astype(jnp.float32)
    label = lax.broadcasted_iota(jnp.int32, table.shape, 1)
    weight = jnp.sum(jnp.where(label == own_ref[0], table, 0.0), axis=1, keepdims=True)
    total = jnp.zeros((count, width), jnp.float32)
    for (k, step), copy in zip(cuts(down_ref), copies["down"]):
        copy.wait()
        total += jnp.dot(hidden[:, k : k + step], down_buf[k : k + step, :], preferred_element_type=jnp.float32)
    out_ref[...] = (total * weight).astype(jnp.bfloat16).reshape(out_ref.shape)


def local(q_latent, q_rope, cache_latent, cache_rope, lengths, tokens_b, routes, gates, w_gate, w_up, w_down):
    latent_width = cache_latent.shape[1]
    requests = lengths.shape[1]
    pool_count = lax.axis_size("pool")
    head_count = lax.axis_size("heads")
    slices = pool_count * head_count // EXPERTS
    own_expert = (lax.axis_index("pool") * head_count + lax.axis_index("heads")) // slices
    token_count, model_width = tokens_b.shape
    table = expert_weights(routes, gates).astype(jnp.bfloat16)
    packed = jnp.concatenate([tokens_b, table], axis=1)
    all_rows = lax.all_to_all(
        jnp.broadcast_to(packed[None], (pool_count,) + packed.shape), "pool", split_axis=0, concat_axis=0, tiled=True
    )
    weights = (w_gate, w_up, w_down)
    terms = pl.pallas_call(
        expert_kernel,
        out_shape=jax.ShapeDtypeStruct((pool_count, token_count, model_width), jnp.bfloat16),
        in_specs=[pl.BlockSpec(memory_space=pltpu.SMEM), pl.BlockSpec(memory_space=pltpu.VMEM)]
        + [pl.BlockSpec(memory_space=pl.ANY)] * 3,
        out_specs=pl.BlockSpec(memory_space=pltpu.VMEM),
        scratch_shapes=[pltpu.VMEM(w.shape, w.dtype) for w in weights]
        + [pltpu.SemaphoreType.DMA((sum(len(cuts(w)) for w in weights),))],
        compiler_params=pltpu.CompilerParams(vmem_limit_bytes=sum(w.size * 2 for w in weights) + (10 << 20)),
    )(
        own_expert.astype(jnp.int32)[None],
        all_rows,
        *[pltpu.with_memory_space_constraint(w, pltpu.HBM) for w in weights],
    )
    terms, q_latent, q_rope, lengths = lax.optimization_barrier((terms, q_latent, q_rope, lengths))
    returned = lax.all_to_all(terms, "pool", split_axis=0, concat_axis=0, tiled=True)
    local_sum = jnp.sum(returned.astype(jnp.float32), axis=0)
    other = lax.ppermute(local_sum, "heads", [(0, 1), (1, 0)])
    moe_out = (local_sum + other).astype(jnp.bfloat16)
    queries = q_latent.reshape(-1, latent_width)
    rope_queries = q_rope.reshape(queries.shape[0], cache_rope.shape[0])
    attended = attend(queries, rope_queries, cache_latent, cache_rope, lengths[0]).reshape(requests, -1)
    return (attended, moe_out)


def solution(mesh):
    rows = P(("groups", "pool"), None)
    split = P(("groups", "pool"), "heads")
    placed = (split, split, rows, P(None, ("groups", "pool")), rows, rows, rows, rows)
    weights = (P(None, ("pool", "heads")),) * 2 + (P(("pool", "heads"), None),)
    return jax.shard_map(
        local, mesh=mesh, in_specs=placed + weights, out_specs=(split, rows), check_vma=False
    )
```

```python
import jax
import jax.numpy as jnp
from jax import lax
from jax.experimental import pallas as pl
from jax.experimental.pallas import tpu as pltpu
from jax.sharding import PartitionSpec as P

EXPERTS = 16
LANES = 128
MIB = 1 << 20

score_scale = 192.0 ** (-0.5)
LOG2E = 1.4426950408889634


def on_chip(count):
    return [pl.BlockSpec(memory_space=pltpu.VMEM)] * count


def in_hbm(array):
    return pltpu.with_memory_space_constraint(array, pltpu.HBM)


def attend_rows(first, count, lengths_ref, q_ref, q_rope_ref, latent_ref, rope_ref, scores, shares):
    rows, total = scores.shape
    heads_here = rows // count
    block = min(256, total)
    position = lax.broadcasted_iota(jnp.int32, (1, total), 1)
    bias, begin = [], jnp.int32(0)
    for r in range(first + count):
        end = begin + lengths_ref[0, r]
        if r >= first:
            bias.append(jnp.where((position >= begin) & (position < end), 0.0, -jnp.inf))
        begin = end
    highest = [jnp.full((heads_here, LANES), -jnp.inf, jnp.float32)] * count
    mine = slice(first * heads_here, first * heads_here + rows)
    for k in range(0, total, block):
        part = lax.dot_general(
            q_ref[mine, :], latent_ref[k : k + block, :], (((1,), (1,)), ((), ())), preferred_element_type=jnp.float32
        ) + jnp.dot(q_rope_ref[mine, :], rope_ref[:, k : k + block], preferred_element_type=jnp.float32)
        for r in range(count):
            own = slice(r * heads_here, (r + 1) * heads_here)
            masked = part[own] + bias[r][:, k : k + block]
            scores[own, k : k + block] = masked
            for j in range(0, block, LANES):
                highest[r] = jnp.maximum(highest[r], masked[:, j : j + LANES])
    scale = score_scale * LOG2E
    for r in range(count):
        own = slice(r * heads_here, (r + 1) * heads_here)
        top = jnp.max(highest[r], axis=1, keepdims=True) * scale
        weights = jnp.exp2(scores[own, :] * scale - top)
        share = 1.0 / jnp.sum(weights, axis=1, keepdims=True)
        shares[own, :] = (weights * share).astype(jnp.bfloat16)
    return jnp.dot(shares[...], latent_ref[...], preferred_element_type=jnp.float32).astype(jnp.bfloat16)


def attend(first, count, queries, rope_queries, latent, rope_keys, lengths, *before):
    requests = lengths.shape[1]
    rows, total = queries.shape[0] // requests * count, latent.shape[0]
    earlier = sum(b.shape[0] for b in before)

    def kernel(lengths_ref, q_ref, q_rope_ref, latent_ref, rope_ref, *refs):
        out_ref, scores, shares = refs[-3:]
        for ref in refs[:-3]:
            out_ref[:earlier, :] = ref[...]
        out_ref[earlier:, :] = attend_rows(
            first, count, lengths_ref, q_ref, q_rope_ref, latent_ref, rope_ref, scores, shares
        )

    return pl.pallas_call(
        kernel,
        out_shape=jax.ShapeDtypeStruct((earlier + rows, queries.shape[1]), jnp.bfloat16),
        in_specs=[pl.BlockSpec(memory_space=pltpu.SMEM)] + on_chip(4 + len(before)),
        out_specs=pl.BlockSpec(memory_space=pltpu.VMEM),
        scratch_shapes=[pltpu.VMEM((rows, total), jnp.float32), pltpu.VMEM((rows, total), jnp.bfloat16)],
        compiler_params=pltpu.CompilerParams(vmem_limit_bytes=14 * MIB),
        cost_estimate=pl.CostEstimate(
            flops=2 * rows * total * 1088, bytes_accessed=4 * MIB, transcendentals=rows * total
        ),
    )(lengths, queries, rope_queries, in_hbm(latent), in_hbm(rope_keys), *before)


def cuts(total, most):
    step = next(s for s in (512, 256, 128, 64, 32, 16) if s <= most and total % s == 0)
    return [(k, step) for k in range(0, total, step)]


def pack_kernel(tokens_ref, routes_ref, gates_ref, out_ref, tokens_buf, routes_buf, gates_buf, sems):
    width = tokens_ref.shape[1]
    copies = [
        pltpu.make_async_copy(source, target, sems.at[k])
        for k, (source, target) in enumerate(
            ((tokens_ref, tokens_buf), (routes_ref, routes_buf), (gates_ref, gates_buf))
        )
    ]
    for copy in copies:
        copy.start()
    for copy in copies[1:]:
        copy.wait()
    label = lax.broadcasted_iota(jnp.int32, (tokens_ref.shape[0], LANES), 1)
    table = jnp.zeros(label.shape, jnp.float32)
    for k in range(routes_ref.shape[1]):
        gate = gates_buf[:, k : k + 1].astype(jnp.float32)
        table += jnp.where(routes_buf[:, k : k + 1] == label, gate, 0.0)
    copies[0].wait()
    for j in range(out_ref.shape[0]):
        out_ref[j, :, :width] = tokens_buf[...]
        out_ref[j, :, width:] = table.astype(jnp.bfloat16)


def pack(tokens, routes, gates, copies):
    return pl.pallas_call(
        pack_kernel,
        out_shape=jax.ShapeDtypeStruct((copies, tokens.shape[0], tokens.shape[1] + LANES), tokens.dtype),
        in_specs=[pl.BlockSpec(memory_space=pl.ANY)] * 3,
        out_specs=pl.BlockSpec(memory_space=pltpu.VMEM),
        scratch_shapes=[
            pltpu.VMEM(tokens.shape, tokens.dtype),
            pltpu.VMEM(routes.shape, routes.dtype),
            pltpu.VMEM(gates.shape, gates.dtype),
            pltpu.SemaphoreType.DMA((3,)),
        ],
        compiler_params=pltpu.CompilerParams(vmem_limit_bytes=8 * MIB),
    )(in_hbm(tokens), in_hbm(routes), in_hbm(gates))


def experts(own_expert, share, shares, rows, w_gate, w_up, w_down):
    width = w_down.shape[1]
    ff = w_down.shape[0] // shares
    thin, wide = cuts(width, 512), cuts(ff, 256)

    def kernel(expert_ref, share_ref, rows_ref, gate_ref, up_ref, down_ref, out_ref, gate_buf, up_buf, down_buf, sems):
        begin = pl.multiple_of(share_ref[0] * ff, ff) if shares > 1 else 0
        copies = [[], [], []]
        for n, (source, target) in enumerate(((gate_ref, gate_buf), (up_ref, up_buf), (down_ref, down_buf))):
            for k, step in wide if n == 2 else thin:
                place = (pl.ds(begin + k, step), slice(None)) if n == 2 else (pl.ds(k, step), pl.ds(begin, ff))
                copy = pltpu.make_async_copy(
                    source.at[place], target.at[pl.ds(k, step)], sems.at[sum(map(len, copies))]
                )
                copy.start()
                copies[n].append(copy)
        count = rows_ref.shape[0] * rows_ref.shape[1]
        packed = rows_ref[...].reshape(count, rows_ref.shape[2])
        table = packed[:, width:].astype(jnp.float32)
        label = lax.broadcasted_iota(jnp.int32, table.shape, 1)
        weight = jnp.sum(jnp.where(label == expert_ref[0], table, 0.0), axis=1, keepdims=True)

        def against(left, parts, waits, buf):
            total = 0.0
            for (k, step), copy in zip(parts, waits):
                copy.wait()
                total += jnp.dot(left[:, k : k + step], buf[k : k + step, :], preferred_element_type=jnp.float32)
            return total

        gate_pre = against(packed, thin, copies[0], gate_buf)
        up_pre = against(packed, thin, copies[1], up_buf)
        hidden = (gate_pre / (1.0 + jnp.exp(-gate_pre)) * up_pre).astype(jnp.bfloat16)
        total = against(hidden, wide, copies[2], down_buf)
        out_ref[...] = (total * weight).astype(jnp.bfloat16).reshape(out_ref.shape)

    return pl.pallas_call(
        kernel,
        out_shape=jax.ShapeDtypeStruct(rows.shape[:2] + (width,), jnp.bfloat16),
        in_specs=[pl.BlockSpec(memory_space=pltpu.SMEM)] * 2
        + on_chip(1)
        + [pl.BlockSpec(memory_space=pl.ANY)] * 3,
        out_specs=pl.BlockSpec(memory_space=pltpu.VMEM),
        scratch_shapes=[
            pltpu.VMEM((width, ff), w_gate.dtype),
            pltpu.VMEM((width, ff), w_up.dtype),
            pltpu.VMEM((ff, width), w_down.dtype),
            pltpu.SemaphoreType.DMA((2 * len(thin) + len(wide),)),
        ],
        compiler_params=pltpu.CompilerParams(vmem_limit_bytes=6 * width * ff + 10 * MIB),
    )(own_expert[None], share[None], rows, in_hbm(w_gate), in_hbm(w_up), in_hbm(w_down))


def local(q_latent, q_rope, cache_latent, cache_rope, lengths, tokens_b, routes, gates, w_gate, w_up, w_down):
    latent_width = cache_latent.shape[1]
    requests = lengths.shape[1]
    pool_count = lax.axis_size("pool")
    head_count = lax.axis_size("heads")
    slices = pool_count * head_count // EXPERTS
    own_pool = lax.axis_index("pool")
    own_expert = (own_pool * head_count + lax.axis_index("heads")) // slices

    group_count = lax.axis_size("groups")
    apart = w_down.shape[0] % (group_count * 256) == 0
    shares, axes = (group_count, ("groups", "pool")) if apart else (1, ("pool",))
    packed = pack(tokens_b, routes, gates, pool_count * shares)
    rows = lax.all_to_all(packed, axes, split_axis=0, concat_axis=0, tiled=True)
    queries = q_latent.reshape(-1, latent_width)
    rope_queries = q_rope.reshape(queries.shape[0], cache_rope.shape[0])
    half = requests // 2
    early = attend(0, half, queries, rope_queries, cache_latent, cache_rope, lengths)
    rows, early, queries, rope_queries = lax.optimization_barrier((rows, early, queries, rope_queries))
    share = lax.axis_index("groups").astype(jnp.int32)
    terms = experts(own_expert, share, shares, rows, w_gate, w_up, w_down)
    terms, queries, rope_queries = lax.optimization_barrier((terms, queries, rope_queries))
    returned = lax.all_to_all(terms, axes, split_axis=0, concat_axis=0, tiled=True)
    attended = attend(half, requests - half, queries, rope_queries, cache_latent, cache_rope, lengths, early)
    attended = attended.reshape(requests, -1)
    returned, attended = lax.optimization_barrier((returned, attended))
    local_sum = jnp.sum(returned.astype(jnp.float32), axis=0)
    other = lax.ppermute(local_sum, "heads", [(0, 1), (1, 0)])
    moe_out = (local_sum + other).astype(jnp.bfloat16)
    return (attended, moe_out)


def solution(mesh):
    rows = P(("groups", "pool"), None)
    split = P(("groups", "pool"), "heads")
    placed = (split, split, rows, P(None, ("groups", "pool")), rows, rows, rows, rows)
    weights = (P(None, ("pool", "heads")),) * 2 + (P(("pool", "heads"), None),)
    return jax.shard_map(
        local, mesh=mesh, in_specs=placed + weights, out_specs=(split, rows), check_vma=False
    )
```

```python
import jax
import jax.numpy as jnp
from jax import lax
from jax.experimental import pallas as pl
from jax.experimental.pallas import tpu as pltpu
from jax.sharding import PartitionSpec as P

EXPERTS = 16
LANES = 128
MIB = 1 << 20
EARLY = 3 * MIB

score_scale = 192.0 ** (-0.5)
LOG2E = 1.4426950408889634


def on_chip(count):
    return [pl.BlockSpec(memory_space=pltpu.VMEM)] * count


def in_hbm(array):
    return pltpu.with_memory_space_constraint(array, pltpu.HBM)


def attend(part, parts, q_latent, q_rope, latent, rope_keys, lengths, done, weight, share, early):
    requests, total, latent_width = lengths.shape[1], latent.shape[0], latent.shape[1]
    rope_width = rope_keys.shape[0]
    heads_here = q_latent.shape[1] // latent_width // parts
    rows = heads_here * requests
    block = min(512, total)
    wide, thin = heads_here * latent_width, heads_here * rope_width
    ff = early[0].shape[1] if early else 0
    chunks = [(k, block) for k in range(0, total, block)]

    def kernel(share_ref, lengths_ref, q_ref, q_rope_ref, latent_ref, rope_ref, *refs):
        rest = len(done) + (1 if early else 0)
        out_ref, piece_refs = refs[rest], refs[rest + 1 : rest + 1 + len(early)]
        (lengths_buf, q_buf, q_rope_buf, latent_buf, rope_buf, tall, tall_rope, scores, out_buf, sems) = refs[
            rest + 1 + len(early) :
        ]
        pairs = [
            (lengths_ref, lengths_buf),
            (q_ref.at[:, pl.ds(part * wide, wide)], q_buf),
            (q_rope_ref.at[:, pl.ds(part * thin, thin)], q_rope_buf),
            (rope_ref, rope_buf),
        ] + [(latent_ref.at[pl.ds(k, n)], latent_buf.at[pl.ds(k, n)]) for k, n in chunks]
        if early:
            begin = pl.multiple_of(share_ref[0] * ff, LANES)
            for k, piece_ref in enumerate(piece_refs):
                n = piece_ref.shape[0]
                pairs.append((refs[len(done)].at[pl.ds(k * n, n), pl.ds(begin, ff)], piece_ref))
        copies = [pltpu.make_async_copy(source, target, sems.at[k]) for k, (source, target) in enumerate(pairs)]
        for copy in copies:
            copy.start()
        for copy in copies[:4]:
            copy.wait()
        for h in range(heads_here):
            own = slice(h * requests, (h + 1) * requests)
            tall[own, :] = q_buf[:, h * latent_width : (h + 1) * latent_width].astype(jnp.float32)
            tall_rope[own, :] = q_rope_buf[:, h * rope_width : (h + 1) * rope_width].astype(jnp.float32)
        queries, rope_queries = tall[...].astype(jnp.bfloat16), tall_rope[...].astype(jnp.bfloat16)
        request = lax.broadcasted_iota(jnp.int32, (requests, 1), 0)
        begin, end, start = jnp.zeros_like(request), jnp.zeros_like(request), jnp.int32(0)
        for r in range(requests):
            begin = jnp.where(request == r, start, begin)
            start = start + lengths_buf[0, r]
            end = jnp.where(request == r, start, end)
        position = lax.broadcasted_iota(jnp.int32, (requests, total), 1)
        bias = jnp.where((position >= begin) & (position < end), 0.0, -jnp.inf)
        highest = jnp.full((heads_here, requests, LANES), -jnp.inf, jnp.float32)
        for (k, n), copy in zip(chunks, copies[4:]):
            copy.wait()
            part_scores = lax.dot_general(
                queries, latent_buf[k : k + n, :], (((1,), (1,)), ((), ())), preferred_element_type=jnp.float32
            ) + jnp.dot(rope_queries, rope_buf[:, k : k + n], preferred_element_type=jnp.float32)
            masked = part_scores.reshape(heads_here, requests, n) + bias[None, :, k : k + n]
            scores[:, k : k + n] = masked.reshape(rows, n)
            for j in range(0, n, LANES):
                highest = jnp.maximum(highest, masked[:, :, j : j + LANES])
        scale = score_scale * LOG2E
        top = jnp.max(highest, axis=2, keepdims=True).reshape(rows, 1) * scale
        step = 64
        for k in range(0, rows, step):
            own = slice(k, k + step)
            weights = jnp.exp2(scores[own, :] * scale - top[own])
            shares = (weights * (1.0 / jnp.sum(weights, axis=1, keepdims=True))).astype(jnp.bfloat16)
            result = jnp.dot(shares, latent_buf[...], preferred_element_type=jnp.float32)
            for j in range(0, step, requests):
                h = (k + j) // requests
                out_buf[:, h * latent_width : (h + 1) * latent_width] = result[j : j + requests].astype(jnp.bfloat16)
        last = pltpu.make_async_copy(out_buf, out_ref.at[:, pl.ds(part * wide, wide)], sems.at[len(pairs)])
        last.start()
        for copy in copies[4 + len(chunks) :]:
            copy.wait()
        last.wait()

    extra = [in_hbm(weight)] if early else []
    return pl.pallas_call(
        kernel,
        out_shape=[pltpu.HBM(q_latent.shape, jnp.bfloat16)] + [pltpu.VMEM(e.shape, e.dtype) for e in early],
        in_specs=[pl.BlockSpec(memory_space=pltpu.SMEM)]
        + [pl.BlockSpec(memory_space=pl.ANY)] * (5 + len(done) + len(extra)),
        out_specs=[pl.BlockSpec(memory_space=pl.ANY)] + on_chip(len(early)),
        input_output_aliases={6: 0} if done else {},
        scratch_shapes=[
            pltpu.SMEM(lengths.shape, lengths.dtype),
            pltpu.VMEM((requests, wide), jnp.bfloat16),
            pltpu.VMEM((requests, thin), jnp.bfloat16),
            pltpu.VMEM(latent.shape, latent.dtype),
            pltpu.VMEM(rope_keys.shape, rope_keys.dtype),
            pltpu.VMEM((rows, latent_width), jnp.float32),
            pltpu.VMEM((rows, rope_width), jnp.float32),
            pltpu.VMEM((rows, total), jnp.float32),
            pltpu.VMEM((requests, wide), jnp.bfloat16),
            pltpu.SemaphoreType.DMA((5 + len(chunks) + len(early),)),
        ],
        compiler_params=pltpu.CompilerParams(vmem_limit_bytes=16 * MIB),
        cost_estimate=pl.CostEstimate(
            flops=2 * rows * total * (2 * latent_width + rope_width),
            bytes_accessed=4 * MIB,
            transcendentals=rows * total,
        ),
    )(share[None], *[in_hbm(x) for x in (lengths, q_latent, q_rope, latent, rope_keys)], *done, *extra)


def cuts(total, most):
    step = next(s for s in (512, 256, 128, 64, 32, 16) if s <= most and total % s == 0)
    return [(k, step) for k in range(0, total, step)]


def pack_kernel(tokens_ref, routes_ref, gates_ref, out_ref, tokens_buf, routes_buf, gates_buf, sems):
    width = tokens_ref.shape[1]
    copies = [
        pltpu.make_async_copy(source, target, sems.at[k])
        for k, (source, target) in enumerate(
            ((tokens_ref, tokens_buf), (routes_ref, routes_buf), (gates_ref, gates_buf))
        )
    ]
    for copy in copies:
        copy.start()
    for copy in copies[1:]:
        copy.wait()
    label = lax.broadcasted_iota(jnp.int32, (tokens_ref.shape[0], LANES), 1)
    table = jnp.zeros(label.shape, jnp.float32)
    for k in range(routes_ref.shape[1]):
        gate = gates_buf[:, k : k + 1].astype(jnp.float32)
        table += jnp.where(routes_buf[:, k : k + 1] == label, gate, 0.0)
    copies[0].wait()
    for j in range(out_ref.shape[0]):
        out_ref[j, :, :width] = tokens_buf[...]
        out_ref[j, :, width:] = table.astype(jnp.bfloat16)


def pack(tokens, routes, gates, copies):
    return pl.pallas_call(
        pack_kernel,
        out_shape=jax.ShapeDtypeStruct((copies, tokens.shape[0], tokens.shape[1] + LANES), tokens.dtype),
        in_specs=[pl.BlockSpec(memory_space=pl.ANY)] * 3,
        out_specs=pl.BlockSpec(memory_space=pltpu.VMEM),
        scratch_shapes=[
            pltpu.VMEM(tokens.shape, tokens.dtype),
            pltpu.VMEM(routes.shape, routes.dtype),
            pltpu.VMEM(gates.shape, gates.dtype),
            pltpu.SemaphoreType.DMA((3,)),
        ],
        compiler_params=pltpu.CompilerParams(vmem_limit_bytes=8 * MIB),
    )(in_hbm(tokens), in_hbm(routes), in_hbm(gates))


def experts(own_expert, share, shares, rows, w_gate, w_up, w_down, early):
    width = w_down.shape[1]
    ff = w_down.shape[0] // shares
    thin, wide = cuts(width, 512), cuts(ff, 256)

    def kernel(expert_ref, share_ref, rows_ref, gate_ref, up_ref, down_ref, *refs):
        early_refs, (out_ref, gate_buf, up_buf, down_buf, out_buf, sems) = refs[: len(early)], refs[len(early) :]
        begin = pl.multiple_of(share_ref[0] * ff, ff) if shares > 1 else 0
        copies = [[], [], []]
        for n, (source, target) in enumerate(((gate_ref, gate_buf), (up_ref, up_buf), (down_ref, down_buf))):
            for k, step in wide if n == 2 else thin[0 if n else len(early) :]:
                place = (pl.ds(begin + k, step), slice(None)) if n == 2 else (pl.ds(k, step), pl.ds(begin, ff))
                copy = pltpu.make_async_copy(
                    source.at[place], target.at[pl.ds(k, step)], sems.at[sum(map(len, copies))]
                )
                copy.start()
                copies[n].append(copy)
        count = rows_ref.shape[0] * rows_ref.shape[1]
        packed = rows_ref[...].reshape(count, rows_ref.shape[2])
        table = packed[:, width:].astype(jnp.float32)
        label = lax.broadcasted_iota(jnp.int32, table.shape, 1)
        weight = jnp.sum(jnp.where(label == expert_ref[0], table, 0.0), axis=1, keepdims=True)

        def against(left, parts, waits, buf):
            total = 0.0
            for (k, step), copy in zip(parts, waits):
                copy.wait()
                total += jnp.dot(left[:, k : k + step], buf[k : k + step, :], preferred_element_type=jnp.float32)
            return total

        gate_pre = 0.0
        for (k, step), ref in zip(thin, early_refs):
            gate_pre += jnp.dot(packed[:, k : k + step], ref[...], preferred_element_type=jnp.float32)
        gate_pre += against(packed, thin[len(early) :], copies[0], gate_buf)
        up_pre = against(packed, thin, copies[1], up_buf)
        hidden = (gate_pre / (1.0 + jnp.exp(-gate_pre)) * up_pre).astype(jnp.bfloat16)
        total = against(hidden, wide, copies[2], down_buf)
        out_buf[...] = (total * weight).astype(jnp.bfloat16).reshape(out_buf.shape)
        last = pltpu.make_async_copy(out_buf, out_ref, sems.at[sum(map(len, copies))])
        last.start()
        last.wait()

    return pl.pallas_call(
        kernel,
        out_shape=pltpu.HBM(rows.shape[:2] + (width,), jnp.bfloat16),
        in_specs=[pl.BlockSpec(memory_space=pltpu.SMEM)] * 2
        + on_chip(1)
        + [pl.BlockSpec(memory_space=pl.ANY)] * 3
        + on_chip(len(early)),
        out_specs=pl.BlockSpec(memory_space=pl.ANY),
        scratch_shapes=[
            pltpu.VMEM((width, ff), w_gate.dtype),
            pltpu.VMEM((width, ff), w_up.dtype),
            pltpu.VMEM((ff, width), w_down.dtype),
            pltpu.VMEM(rows.shape[:2] + (width,), jnp.bfloat16),
            pltpu.SemaphoreType.DMA((2 * len(thin) + len(wide) + 1,)),
        ],
        compiler_params=pltpu.CompilerParams(vmem_limit_bytes=6 * width * ff + 10 * MIB),
    )(own_expert[None], share[None], rows, in_hbm(w_gate), in_hbm(w_up), in_hbm(w_down), *early)


def local(q_latent, q_rope, cache_latent, cache_rope, lengths, tokens_b, routes, gates, w_gate, w_up, w_down):
    pool_count = lax.axis_size("pool")
    head_count = lax.axis_size("heads")
    slices = pool_count * head_count // EXPERTS
    own_pool = lax.axis_index("pool")
    own_expert = (own_pool * head_count + lax.axis_index("heads")) // slices

    group_count = lax.axis_size("groups")
    apart = w_down.shape[0] % (group_count * 256) == 0
    shares, axes = (group_count, ("groups", "pool")) if apart else (1, ("pool",))
    packed = pack(tokens_b, routes, gates, pool_count * shares)
    rows = lax.all_to_all(packed, axes, split_axis=0, concat_axis=0, tiled=True)
    share = lax.axis_index("groups").astype(jnp.int32) if apart else jnp.int32(0)
    ff = w_down.shape[0] // shares
    model_width = tokens_b.shape[1]
    step = cuts(model_width, 512)[0][1]
    pieces = min(model_width // step, EARLY // (2 * step * ff))
    pieces = [jax.ShapeDtypeStruct((step, ff), w_gate.dtype)] * pieces
    inputs = (q_latent, q_rope, cache_latent, cache_rope, lengths)
    half, *early = attend(0, 2, *inputs, [], w_gate, share, pieces)
    rows, half, *early = lax.optimization_barrier((rows, half, *early))
    terms = experts(own_expert, share, shares, rows, w_gate, w_up, w_down, early)
    terms, half = lax.optimization_barrier((terms, half))
    returned = lax.all_to_all(terms, axes, split_axis=0, concat_axis=0, tiled=True)
    (attended,) = attend(1, 2, *inputs, [half], w_gate, share, [])
    returned, attended = lax.optimization_barrier((returned, attended))
    local_sum = jnp.sum(returned.astype(jnp.float32), axis=0)
    other = lax.ppermute(local_sum, "heads", [(0, 1), (1, 0)])
    moe_out = (local_sum + other).astype(jnp.bfloat16)
    return (attended, moe_out)


def solution(mesh):
    rows = P(("groups", "pool"), None)
    split = P(("groups", "pool"), "heads")
    placed = (split, split, rows, P(None, ("groups", "pool")), rows, rows, rows, rows)
    weights = (P(None, ("pool", "heads")),) * 2 + (P(("pool", "heads"), None),)
    return jax.shard_map(
        local, mesh=mesh, in_specs=placed + weights, out_specs=(split, rows), check_vma=False
    )
```

```python
import jax
import jax.numpy as jnp
from jax import lax
from jax.experimental import pallas as pl
from jax.experimental.pallas import tpu as pltpu
from jax.sharding import PartitionSpec as P

EXPERTS = 16
LANES = 128
MIB = 1 << 20
EARLY = 3 * MIB

score_scale = 192.0 ** (-0.5)
LOG2E = 1.4426950408889634


def on_chip(count):
    return [pl.BlockSpec(memory_space=pltpu.VMEM)] * count


def in_hbm(array):
    return pltpu.with_memory_space_constraint(array, pltpu.HBM)


def attend(part, parts, q_latent, q_rope, latent, rope_keys, lengths, done, weight, share, early):
    requests, total, latent_width = lengths.shape[1], latent.shape[0], latent.shape[1]
    rope_width = rope_keys.shape[0]
    heads_here = q_latent.shape[1] // latent_width // parts
    rows = heads_here * requests
    block = min(512, total)
    wide, thin = heads_here * latent_width, heads_here * rope_width
    ff = early[0].shape[1] if early else 0
    chunks = [(k, block) for k in range(0, total, block)]

    def kernel(share_ref, lengths_ref, q_ref, q_rope_ref, latent_ref, rope_ref, *refs):
        rest = len(done) + (1 if early else 0)
        out_ref, piece_refs = refs[rest], refs[rest + 1 : rest + 1 + len(early)]
        (lengths_buf, q_buf, q_rope_buf, latent_buf, rope_buf, tall, tall_rope, scores, out_buf, sems) = refs[
            rest + 1 + len(early) :
        ]
        pairs = [
            (lengths_ref, lengths_buf),
            (q_ref.at[:, pl.ds(part * wide, wide)], q_buf),
            (q_rope_ref.at[:, pl.ds(part * thin, thin)], q_rope_buf),
            (rope_ref, rope_buf),
        ] + [(latent_ref.at[pl.ds(k, n)], latent_buf.at[pl.ds(k, n)]) for k, n in chunks]
        if early:
            begin = pl.multiple_of(share_ref[0] * ff, LANES)
            for k, piece_ref in enumerate(piece_refs):
                n = piece_ref.shape[0]
                pairs.append((refs[len(done)].at[pl.ds(k * n, n), pl.ds(begin, ff)], piece_ref))
        copies = [pltpu.make_async_copy(source, target, sems.at[k]) for k, (source, target) in enumerate(pairs)]
        for copy in copies:
            copy.start()
        for copy in copies[:4]:
            copy.wait()
        for h in range(heads_here):
            own = slice(h * requests, (h + 1) * requests)
            tall[own, :] = q_buf[:, h * latent_width : (h + 1) * latent_width].astype(jnp.float32)
            tall_rope[own, :] = q_rope_buf[:, h * rope_width : (h + 1) * rope_width].astype(jnp.float32)
        queries, rope_queries = tall[...].astype(jnp.bfloat16), tall_rope[...].astype(jnp.bfloat16)
        request = lax.broadcasted_iota(jnp.int32, (requests, 1), 0)
        begin, end, start = jnp.zeros_like(request), jnp.zeros_like(request), jnp.int32(0)
        for r in range(requests):
            begin = jnp.where(request == r, start, begin)
            start = start + lengths_buf[0, r]
            end = jnp.where(request == r, start, end)
        position = lax.broadcasted_iota(jnp.int32, (requests, total), 1)
        bias = jnp.where((position >= begin) & (position < end), 0.0, -jnp.inf)
        highest = jnp.full((heads_here, requests, LANES), -jnp.inf, jnp.float32)
        for (k, n), copy in zip(chunks, copies[4:]):
            copy.wait()
            part_scores = lax.dot_general(
                queries, latent_buf[k : k + n, :], (((1,), (1,)), ((), ())), preferred_element_type=jnp.float32
            ) + jnp.dot(rope_queries, rope_buf[:, k : k + n], preferred_element_type=jnp.float32)
            masked = part_scores.reshape(heads_here, requests, n) + bias[None, :, k : k + n]
            scores[:, k : k + n] = masked.reshape(rows, n)
            for j in range(0, n, LANES):
                highest = jnp.maximum(highest, masked[:, :, j : j + LANES])
        scale = score_scale * LOG2E
        top = jnp.max(highest, axis=2, keepdims=True).reshape(rows, 1) * scale
        step = 64
        for k in range(0, rows, step):
            own = slice(k, k + step)
            weights = jnp.exp2(scores[own, :] * scale - top[own])
            shares = (weights * (1.0 / jnp.sum(weights, axis=1, keepdims=True))).astype(jnp.bfloat16)
            result = jnp.dot(shares, latent_buf[...], preferred_element_type=jnp.float32)
            for j in range(0, step, requests):
                h = (k + j) // requests
                out_buf[:, h * latent_width : (h + 1) * latent_width] = result[j : j + requests].astype(jnp.bfloat16)
        last = pltpu.make_async_copy(out_buf, out_ref.at[:, pl.ds(part * wide, wide)], sems.at[len(pairs)])
        last.start()
        for copy in copies[4 + len(chunks) :]:
            copy.wait()
        last.wait()

    extra = [in_hbm(weight)] if early else []
    return pl.pallas_call(
        kernel,
        out_shape=[pltpu.HBM(q_latent.shape, jnp.bfloat16)] + [pltpu.VMEM(e.shape, e.dtype) for e in early],
        in_specs=[pl.BlockSpec(memory_space=pltpu.SMEM)]
        + [pl.BlockSpec(memory_space=pl.ANY)] * (5 + len(done) + len(extra)),
        out_specs=[pl.BlockSpec(memory_space=pl.ANY)] + on_chip(len(early)),
        input_output_aliases={6: 0} if done else {},
        scratch_shapes=[
            pltpu.SMEM(lengths.shape, lengths.dtype),
            pltpu.VMEM((requests, wide), jnp.bfloat16),
            pltpu.VMEM((requests, thin), jnp.bfloat16),
            pltpu.VMEM(latent.shape, latent.dtype),
            pltpu.VMEM(rope_keys.shape, rope_keys.dtype),
            pltpu.VMEM((rows, latent_width), jnp.float32),
            pltpu.VMEM((rows, rope_width), jnp.float32),
            pltpu.VMEM((rows, total), jnp.float32),
            pltpu.VMEM((requests, wide), jnp.bfloat16),
            pltpu.SemaphoreType.DMA((5 + len(chunks) + len(early),)),
        ],
        compiler_params=pltpu.CompilerParams(vmem_limit_bytes=16 * MIB),
        cost_estimate=pl.CostEstimate(
            flops=2 * rows * total * (2 * latent_width + rope_width),
            bytes_accessed=4 * MIB,
            transcendentals=rows * total,
        ),
    )(share[None], *[in_hbm(x) for x in (lengths, q_latent, q_rope, latent, rope_keys)], *done, *extra)


def cuts(total, most):
    step = next(s for s in (512, 256, 128, 64, 32, 16) if s <= most and total % s == 0)
    return [(k, step) for k in range(0, total, step)]


def pack_kernel(tokens_ref, routes_ref, gates_ref, out_ref, tokens_buf, routes_buf, gates_buf, sems):
    width = tokens_ref.shape[1]
    copies = [
        pltpu.make_async_copy(source, target, sems.at[k])
        for k, (source, target) in enumerate(
            ((tokens_ref, tokens_buf), (routes_ref, routes_buf), (gates_ref, gates_buf))
        )
    ]
    for copy in copies:
        copy.start()
    for copy in copies[1:]:
        copy.wait()
    label = lax.broadcasted_iota(jnp.int32, (tokens_ref.shape[0], LANES), 1)
    table = jnp.zeros(label.shape, jnp.float32)
    for k in range(routes_ref.shape[1]):
        gate = gates_buf[:, k : k + 1].astype(jnp.float32)
        table += jnp.where(routes_buf[:, k : k + 1] == label, gate, 0.0)
    copies[0].wait()
    for j in range(out_ref.shape[0]):
        out_ref[j, :, :width] = tokens_buf[...]
        out_ref[j, :, width:] = table.astype(jnp.bfloat16)


def pack(tokens, routes, gates, copies):
    return pl.pallas_call(
        pack_kernel,
        out_shape=jax.ShapeDtypeStruct((copies, tokens.shape[0], tokens.shape[1] + LANES), tokens.dtype),
        in_specs=[pl.BlockSpec(memory_space=pl.ANY)] * 3,
        out_specs=pl.BlockSpec(memory_space=pltpu.VMEM),
        scratch_shapes=[
            pltpu.VMEM(tokens.shape, tokens.dtype),
            pltpu.VMEM(routes.shape, routes.dtype),
            pltpu.VMEM(gates.shape, gates.dtype),
            pltpu.SemaphoreType.DMA((3,)),
        ],
        compiler_params=pltpu.CompilerParams(vmem_limit_bytes=8 * MIB),
    )(in_hbm(tokens), in_hbm(routes), in_hbm(gates))


def experts(own_expert, share, shares, rows, w_gate, w_up, w_down, early):
    width = w_down.shape[1]
    ff = w_down.shape[0] // shares
    thin, wide = cuts(width, 512), cuts(ff, 256)

    def kernel(expert_ref, share_ref, rows_ref, gate_ref, up_ref, down_ref, *refs):
        early_refs, (out_ref, gate_buf, up_buf, down_buf, out_buf, sems) = refs[: len(early)], refs[len(early) :]
        begin = pl.multiple_of(share_ref[0] * ff, ff) if shares > 1 else 0
        copies = [[], [], []]
        for n, (source, target) in enumerate(((gate_ref, gate_buf), (up_ref, up_buf), (down_ref, down_buf))):
            for k, step in wide if n == 2 else thin[0 if n else len(early) :]:
                place = (pl.ds(begin + k, step), slice(None)) if n == 2 else (pl.ds(k, step), pl.ds(begin, ff))
                copy = pltpu.make_async_copy(
                    source.at[place], target.at[pl.ds(k, step)], sems.at[sum(map(len, copies))]
                )
                copy.start()
                copies[n].append(copy)
        count = rows_ref.shape[0] * rows_ref.shape[1]
        packed = rows_ref[...].reshape(count, rows_ref.shape[2])
        table = packed[:, width:].astype(jnp.float32)
        label = lax.broadcasted_iota(jnp.int32, table.shape, 1)
        weight = jnp.sum(jnp.where(label == expert_ref[0], table, 0.0), axis=1, keepdims=True)

        def against(left, parts, waits, buf):
            total = 0.0
            for (k, step), copy in zip(parts, waits):
                copy.wait()
                total += jnp.dot(left[:, k : k + step], buf[k : k + step, :], preferred_element_type=jnp.float32)
            return total

        gate_pre = 0.0
        for (k, step), ref in zip(thin, early_refs):
            gate_pre += jnp.dot(packed[:, k : k + step], ref[...], preferred_element_type=jnp.float32)
        gate_pre += against(packed, thin[len(early) :], copies[0], gate_buf)
        up_pre = against(packed, thin, copies[1], up_buf)
        hidden = (gate_pre / (1.0 + jnp.exp(-gate_pre)) * up_pre).astype(jnp.bfloat16)
        total = against(hidden, wide, copies[2], down_buf)
        out_buf[...] = (total * weight).astype(jnp.bfloat16).reshape(out_buf.shape)
        last = pltpu.make_async_copy(out_buf, out_ref, sems.at[sum(map(len, copies))])
        last.start()
        last.wait()

    return pl.pallas_call(
        kernel,
        out_shape=pltpu.HBM(rows.shape[:2] + (width,), jnp.bfloat16),
        in_specs=[pl.BlockSpec(memory_space=pltpu.SMEM)] * 2
        + on_chip(1)
        + [pl.BlockSpec(memory_space=pl.ANY)] * 3
        + on_chip(len(early)),
        out_specs=pl.BlockSpec(memory_space=pl.ANY),
        scratch_shapes=[
            pltpu.VMEM((width, ff), w_gate.dtype),
            pltpu.VMEM((width, ff), w_up.dtype),
            pltpu.VMEM((ff, width), w_down.dtype),
            pltpu.VMEM(rows.shape[:2] + (width,), jnp.bfloat16),
            pltpu.SemaphoreType.DMA((2 * len(thin) + len(wide) + 1,)),
        ],
        compiler_params=pltpu.CompilerParams(vmem_limit_bytes=6 * width * ff + 10 * MIB),
    )(own_expert[None], share[None], rows, in_hbm(w_gate), in_hbm(w_up), in_hbm(w_down), *early)


def local(q_latent, q_rope, cache_latent, cache_rope, lengths, tokens_b, routes, gates, w_gate, w_up, w_down):
    pool_count = lax.axis_size("pool")
    head_count = lax.axis_size("heads")
    slices = pool_count * head_count // EXPERTS
    own_pool = lax.axis_index("pool")
    own_expert = (own_pool * head_count + lax.axis_index("heads")) // slices

    group_count = lax.axis_size("groups")
    apart = w_down.shape[0] % (group_count * 256) == 0
    shares, axes = (group_count, ("groups", "pool")) if apart else (1, ("pool",))
    peers = pool_count * shares
    middle = peers * 3 // 4
    order = [middle] + [i for i in reversed(range(peers)) if i != middle]

    def swap(blocks):
        return lax.all_to_all(blocks, axes, split_axis=0, concat_axis=0, tiled=True, axis_index_groups=[order])

    rows = swap(pack(tokens_b, routes, gates, peers))
    share = lax.axis_index("groups").astype(jnp.int32) if apart else jnp.int32(0)
    ff = w_down.shape[0] // shares
    model_width = tokens_b.shape[1]
    step = cuts(model_width, 512)[0][1]
    pieces = min(model_width // step, EARLY // (2 * step * ff))
    pieces = [jax.ShapeDtypeStruct((step, ff), w_gate.dtype)] * pieces
    inputs = (q_latent, q_rope, cache_latent, cache_rope, lengths)
    half, *early = attend(0, 2, *inputs, [], w_gate, share, pieces)
    rows, half, *early = lax.optimization_barrier((rows, half, *early))
    terms = experts(own_expert, share, shares, rows, w_gate, w_up, w_down, early)
    terms, half = lax.optimization_barrier((terms, half))
    returned = swap(terms)
    (attended,) = attend(1, 2, *inputs, [half], w_gate, share, [])
    returned, attended = lax.optimization_barrier((returned, attended))
    local_sum = jnp.sum(returned.astype(jnp.float32), axis=0)
    other = lax.ppermute(local_sum, "heads", [(0, 1), (1, 0)])
    moe_out = (local_sum + other).astype(jnp.bfloat16)
    return (attended, moe_out)


def solution(mesh):
    rows = P(("groups", "pool"), None)
    split = P(("groups", "pool"), "heads")
    placed = (split, split, rows, P(None, ("groups", "pool")), rows, rows, rows, rows)
    weights = (P(None, ("pool", "heads")),) * 2 + (P(("pool", "heads"), None),)
    return jax.shard_map(
        local, mesh=mesh, in_specs=placed + weights, out_specs=(split, rows), check_vma=False
    )
```

```python
import jax
import jax.numpy as jnp
from jax import lax
from jax.experimental import pallas as pl
from jax.experimental.pallas import tpu as pltpu
from jax.sharding import PartitionSpec as P

EXPERTS = 16
LANES = 128
MIB = 1 << 20
EARLY = 3 * MIB

score_scale = 192.0 ** (-0.5)
LOG2E = 1.4426950408889634


def on_chip(count):
    return [pl.BlockSpec(memory_space=pltpu.VMEM)] * count


def in_hbm(array):
    return pltpu.with_memory_space_constraint(array, pltpu.HBM)


def attend(part, parts, q_latent, q_rope, latent, rope_keys, lengths, done, weight, share, early):
    requests, total, latent_width = lengths.shape[1], latent.shape[0], latent.shape[1]
    rope_width = rope_keys.shape[0]
    heads_here = q_latent.shape[1] // latent_width // parts
    rows = heads_here * requests
    block = min(1024, total)
    wide, thin = heads_here * latent_width, heads_here * rope_width
    ff = early[0].shape[1] if early else 0
    chunks = [(k, block) for k in range(0, total, block)]

    def kernel(share_ref, lengths_ref, q_ref, q_rope_ref, latent_ref, rope_ref, *refs):
        rest = len(done) + (1 if early else 0)
        out_ref, piece_refs = refs[rest], refs[rest + 1 : rest + 1 + len(early)]
        (lengths_buf, q_buf, q_rope_buf, latent_buf, rope_buf, tall, tall_rope, scores, out_buf, sems) = refs[
            rest + 1 + len(early) :
        ]
        pairs = [
            (lengths_ref, lengths_buf),
            (q_ref.at[:, pl.ds(part * wide, wide)], q_buf),
            (q_rope_ref.at[:, pl.ds(part * thin, thin)], q_rope_buf),
            (rope_ref, rope_buf),
        ] + [(latent_ref.at[pl.ds(k, n)], latent_buf.at[pl.ds(k, n)]) for k, n in chunks]
        if early:
            begin = pl.multiple_of(share_ref[0] * ff, LANES)
            for k, piece_ref in enumerate(piece_refs):
                n = piece_ref.shape[0]
                pairs.append((refs[len(done)].at[pl.ds(k * n, n), pl.ds(begin, ff)], piece_ref))
        copies = [pltpu.make_async_copy(source, target, sems.at[k]) for k, (source, target) in enumerate(pairs)]
        for copy in copies:
            copy.start()
        for copy in copies[:4]:
            copy.wait()
        for h in range(heads_here):
            own = slice(h * requests, (h + 1) * requests)
            tall[own, :] = q_buf[:, h * latent_width : (h + 1) * latent_width].astype(jnp.float32)
            tall_rope[own, :] = q_rope_buf[:, h * rope_width : (h + 1) * rope_width].astype(jnp.float32)
        queries, rope_queries = tall[...].astype(jnp.bfloat16), tall_rope[...].astype(jnp.bfloat16)
        request = lax.broadcasted_iota(jnp.int32, (requests, 1), 0)
        begin, end, start = jnp.zeros_like(request), jnp.zeros_like(request), jnp.int32(0)
        for r in range(requests):
            begin = jnp.where(request == r, start, begin)
            start = start + lengths_buf[0, r]
            end = jnp.where(request == r, start, end)
        position = lax.broadcasted_iota(jnp.int32, (requests, total), 1)
        bias = jnp.where((position >= begin) & (position < end), 0.0, -jnp.inf)
        highest = jnp.full((heads_here, requests, LANES), -jnp.inf, jnp.float32)
        for (k, n), copy in zip(chunks, copies[4:]):
            copy.wait()
            part_scores = lax.dot_general(
                queries, latent_buf[k : k + n, :], (((1,), (1,)), ((), ())), preferred_element_type=jnp.float32
            ) + jnp.dot(rope_queries, rope_buf[:, k : k + n], preferred_element_type=jnp.float32)
            masked = part_scores.reshape(heads_here, requests, n) + bias[None, :, k : k + n]
            scores[:, k : k + n] = masked.reshape(rows, n)
            for j in range(0, n, LANES):
                highest = jnp.maximum(highest, masked[:, :, j : j + LANES])
        scale = score_scale * LOG2E
        top = jnp.max(highest, axis=2, keepdims=True).reshape(rows, 1) * scale
        step = min(rows, 256)
        for k in range(0, rows, step):
            own = slice(k, k + step)
            weights = jnp.exp2(scores[own, :] * scale - top[own])
            whole = 1.0 / jnp.sum(weights, axis=1, keepdims=True)
            result = jnp.dot(weights.astype(jnp.bfloat16), latent_buf[...], preferred_element_type=jnp.float32) * whole
            for j in range(0, step, requests):
                h = (k + j) // requests
                out_buf[:, h * latent_width : (h + 1) * latent_width] = result[j : j + requests].astype(jnp.bfloat16)
        last = pltpu.make_async_copy(out_buf, out_ref.at[:, pl.ds(part * wide, wide)], sems.at[len(pairs)])
        last.start()
        for copy in copies[4 + len(chunks) :]:
            copy.wait()
        last.wait()

    extra = [in_hbm(weight)] if early else []
    return pl.pallas_call(
        kernel,
        out_shape=[pltpu.HBM(q_latent.shape, jnp.bfloat16)] + [pltpu.VMEM(e.shape, e.dtype) for e in early],
        in_specs=[pl.BlockSpec(memory_space=pltpu.SMEM)]
        + [pl.BlockSpec(memory_space=pl.ANY)] * (5 + len(done) + len(extra)),
        out_specs=[pl.BlockSpec(memory_space=pl.ANY)] + on_chip(len(early)),
        input_output_aliases={6: 0} if done else {},
        scratch_shapes=[
            pltpu.SMEM(lengths.shape, lengths.dtype),
            pltpu.VMEM((requests, wide), jnp.bfloat16),
            pltpu.VMEM((requests, thin), jnp.bfloat16),
            pltpu.VMEM(latent.shape, latent.dtype),
            pltpu.VMEM(rope_keys.shape, rope_keys.dtype),
            pltpu.VMEM((rows, latent_width), jnp.float32),
            pltpu.VMEM((rows, rope_width), jnp.float32),
            pltpu.VMEM((rows, total), jnp.float32),
            pltpu.VMEM((requests, wide), jnp.bfloat16),
            pltpu.SemaphoreType.DMA((5 + len(chunks) + len(early),)),
        ],
        compiler_params=pltpu.CompilerParams(vmem_limit_bytes=16 * MIB),
        cost_estimate=pl.CostEstimate(
            flops=2 * rows * total * (2 * latent_width + rope_width),
            bytes_accessed=4 * MIB,
            transcendentals=rows * total,
        ),
    )(share[None], *[in_hbm(x) for x in (lengths, q_latent, q_rope, latent, rope_keys)], *done, *extra)


def cuts(total, most):
    step = next(s for s in (512, 256, 128, 64, 32, 16) if s <= most and total % s == 0)
    return [(k, step) for k in range(0, total, step)]


def pack_kernel(tokens_ref, routes_ref, gates_ref, out_ref, tokens_buf, routes_buf, gates_buf, sems):
    width = tokens_ref.shape[1]
    copies = [
        pltpu.make_async_copy(source, target, sems.at[k])
        for k, (source, target) in enumerate(
            ((tokens_ref, tokens_buf), (routes_ref, routes_buf), (gates_ref, gates_buf))
        )
    ]
    for copy in copies:
        copy.start()
    for copy in copies[1:]:
        copy.wait()
    label = lax.broadcasted_iota(jnp.int32, (tokens_ref.shape[0], LANES), 1)
    table = jnp.zeros(label.shape, jnp.float32)
    for k in range(routes_ref.shape[1]):
        gate = gates_buf[:, k : k + 1].astype(jnp.float32)
        table += jnp.where(routes_buf[:, k : k + 1] == label, gate, 0.0)
    copies[0].wait()
    for j in range(out_ref.shape[0]):
        out_ref[j, :, :width] = tokens_buf[...]
        out_ref[j, :, width:] = table.astype(jnp.bfloat16)


def pack(tokens, routes, gates, copies):
    return pl.pallas_call(
        pack_kernel,
        out_shape=jax.ShapeDtypeStruct((copies, tokens.shape[0], tokens.shape[1] + LANES), tokens.dtype),
        in_specs=[pl.BlockSpec(memory_space=pl.ANY)] * 3,
        out_specs=pl.BlockSpec(memory_space=pltpu.VMEM),
        scratch_shapes=[
            pltpu.VMEM(tokens.shape, tokens.dtype),
            pltpu.VMEM(routes.shape, routes.dtype),
            pltpu.VMEM(gates.shape, gates.dtype),
            pltpu.SemaphoreType.DMA((3,)),
        ],
        compiler_params=pltpu.CompilerParams(vmem_limit_bytes=8 * MIB),
    )(in_hbm(tokens), in_hbm(routes), in_hbm(gates))


def experts(own_expert, share, shares, rows, w_gate, w_up, w_down, early):
    width = w_down.shape[1]
    ff = w_down.shape[0] // shares
    thin, wide = cuts(width, 512), cuts(ff, 256)

    def kernel(expert_ref, share_ref, rows_ref, gate_ref, up_ref, down_ref, *refs):
        early_refs, (out_ref, gate_buf, up_buf, down_buf, out_buf, sems) = refs[: len(early)], refs[len(early) :]
        begin = pl.multiple_of(share_ref[0] * ff, ff) if shares > 1 else 0
        copies = [[], [], []]
        for n, (source, target) in enumerate(((gate_ref, gate_buf), (up_ref, up_buf), (down_ref, down_buf))):
            for k, step in wide if n == 2 else thin[0 if n else len(early) :]:
                place = (pl.ds(begin + k, step), slice(None)) if n == 2 else (pl.ds(k, step), pl.ds(begin, ff))
                copy = pltpu.make_async_copy(
                    source.at[place], target.at[pl.ds(k, step)], sems.at[sum(map(len, copies))]
                )
                copy.start()
                copies[n].append(copy)
        count = rows_ref.shape[0] * rows_ref.shape[1]
        packed = rows_ref[...].reshape(count, rows_ref.shape[2])
        table = packed[:, width:].astype(jnp.float32)
        label = lax.broadcasted_iota(jnp.int32, table.shape, 1)
        weight = jnp.sum(jnp.where(label == expert_ref[0], table, 0.0), axis=1, keepdims=True)

        def against(left, parts, waits, buf):
            total = 0.0
            for (k, step), copy in zip(parts, waits):
                copy.wait()
                total += jnp.dot(left[:, k : k + step], buf[k : k + step, :], preferred_element_type=jnp.float32)
            return total

        gate_pre = 0.0
        for (k, step), ref in zip(thin, early_refs):
            gate_pre += jnp.dot(packed[:, k : k + step], ref[...], preferred_element_type=jnp.float32)
        gate_pre += against(packed, thin[len(early) :], copies[0], gate_buf)
        up_pre = against(packed, thin, copies[1], up_buf)
        hidden = (gate_pre / (1.0 + jnp.exp(-gate_pre)) * up_pre).astype(jnp.bfloat16)
        total = against(hidden, wide, copies[2], down_buf)
        out_buf[...] = (total * weight).astype(jnp.bfloat16).reshape(out_buf.shape)
        last = pltpu.make_async_copy(out_buf, out_ref, sems.at[sum(map(len, copies))])
        last.start()
        last.wait()

    return pl.pallas_call(
        kernel,
        out_shape=pltpu.HBM(rows.shape[:2] + (width,), jnp.bfloat16),
        in_specs=[pl.BlockSpec(memory_space=pltpu.SMEM)] * 2
        + on_chip(1)
        + [pl.BlockSpec(memory_space=pl.ANY)] * 3
        + on_chip(len(early)),
        out_specs=pl.BlockSpec(memory_space=pl.ANY),
        scratch_shapes=[
            pltpu.VMEM((width, ff), w_gate.dtype),
            pltpu.VMEM((width, ff), w_up.dtype),
            pltpu.VMEM((ff, width), w_down.dtype),
            pltpu.VMEM(rows.shape[:2] + (width,), jnp.bfloat16),
            pltpu.SemaphoreType.DMA((2 * len(thin) + len(wide) + 1,)),
        ],
        compiler_params=pltpu.CompilerParams(vmem_limit_bytes=6 * width * ff + 10 * MIB),
    )(own_expert[None], share[None], rows, in_hbm(w_gate), in_hbm(w_up), in_hbm(w_down), *early)


def local(q_latent, q_rope, cache_latent, cache_rope, lengths, tokens_b, routes, gates, w_gate, w_up, w_down):
    pool_count = lax.axis_size("pool")
    head_count = lax.axis_size("heads")
    slices = pool_count * head_count // EXPERTS
    own_pool = lax.axis_index("pool")
    own_expert = (own_pool * head_count + lax.axis_index("heads")) // slices

    group_count = lax.axis_size("groups")
    apart = w_down.shape[0] % (group_count * 256) == 0
    shares, axes = (group_count, ("groups", "pool")) if apart else (1, ("pool",))
    peers = pool_count * shares
    middle = peers * 3 // 4
    order = [middle] + [i for i in reversed(range(peers)) if i != middle]

    def swap(blocks):
        return lax.all_to_all(blocks, axes, split_axis=0, concat_axis=0, tiled=True, axis_index_groups=[order])

    rows = swap(pack(tokens_b, routes, gates, peers))
    share = lax.axis_index("groups").astype(jnp.int32) if apart else jnp.int32(0)
    ff = w_down.shape[0] // shares
    model_width = tokens_b.shape[1]
    step = cuts(model_width, 512)[0][1]
    pieces = min(model_width // step, EARLY // (2 * step * ff))
    pieces = [jax.ShapeDtypeStruct((step, ff), w_gate.dtype)] * pieces
    inputs = (q_latent, q_rope, cache_latent, cache_rope, lengths)
    half, *early = attend(0, 2, *inputs, [], w_gate, share, pieces)
    rows, half, *early = lax.optimization_barrier((rows, half, *early))
    terms = experts(own_expert, share, shares, rows, w_gate, w_up, w_down, early)
    terms, half = lax.optimization_barrier((terms, half))
    returned = swap(terms)
    (attended,) = attend(1, 2, *inputs, [half], w_gate, share, [])
    returned, attended = lax.optimization_barrier((returned, attended))
    local_sum = jnp.sum(returned.astype(jnp.float32), axis=0)
    other = lax.ppermute(local_sum, "heads", [(0, 1), (1, 0)])
    moe_out = (local_sum + other).astype(jnp.bfloat16)
    return (attended, moe_out)


def solution(mesh):
    rows = P(("groups", "pool"), None)
    split = P(("groups", "pool"), "heads")
    placed = (split, split, rows, P(None, ("groups", "pool")), rows, rows, rows, rows)
    weights = (P(None, ("pool", "heads")),) * 2 + (P(("pool", "heads"), None),)
    return jax.shard_map(
        local, mesh=mesh, in_specs=placed + weights, out_specs=(split, rows), check_vma=False
    )
```

```python
import jax
import jax.numpy as jnp
from jax import lax
from jax.experimental import pallas as pl
from jax.experimental.pallas import tpu as pltpu
from jax.sharding import PartitionSpec as P

EXPERTS = 16
LANES = 128
MIB = 1 << 20
EARLY = 3 * MIB

score_scale = 192.0 ** (-0.5)
LOG2E = 1.4426950408889634


def on_chip(count):
    return [pl.BlockSpec(memory_space=pltpu.VMEM)] * count


def in_hbm(array):
    return pltpu.with_memory_space_constraint(array, pltpu.HBM)


def attend(part, parts, q_latent, q_rope, latent, rope_keys, lengths, done, weight, share, early):
    requests, total, latent_width = lengths.shape[1], latent.shape[0], latent.shape[1]
    rope_width = rope_keys.shape[0]
    heads_here = q_latent.shape[1] // latent_width // parts
    rows = heads_here * requests
    block = min(1024, total)
    wide, thin = heads_here * latent_width, heads_here * rope_width
    ff = early[0].shape[1] if early else 0
    chunks = [(k, block) for k in range(0, total, block)]

    def kernel(share_ref, lengths_ref, q_ref, q_rope_ref, latent_ref, rope_ref, *refs):
        rest = len(done) + (1 if early else 0)
        out_ref, piece_refs = refs[rest], refs[rest + 1 : rest + 1 + len(early)]
        (lengths_buf, q_buf, q_rope_buf, latent_buf, rope_buf, tall, tall_rope, scores, out_buf, sems) = refs[
            rest + 1 + len(early) :
        ]
        pairs = [
            (lengths_ref, lengths_buf),
            (q_ref.at[:, pl.ds(part * wide, wide)], q_buf),
            (q_rope_ref.at[:, pl.ds(part * thin, thin)], q_rope_buf),
            (rope_ref, rope_buf),
        ] + [(latent_ref.at[pl.ds(k, n)], latent_buf.at[pl.ds(k, n)]) for k, n in chunks]
        if early:
            begin = pl.multiple_of(share_ref[0] * ff, LANES)
            for k, piece_ref in enumerate(piece_refs):
                n = piece_ref.shape[0]
                pairs.append((refs[len(done)].at[pl.ds(k * n, n), pl.ds(begin, ff)], piece_ref))
        copies = [pltpu.make_async_copy(source, target, sems.at[k]) for k, (source, target) in enumerate(pairs)]
        for copy in copies:
            copy.start()
        for copy in copies[:4]:
            copy.wait()
        for h in range(heads_here):
            own = slice(h * requests, (h + 1) * requests)
            tall[own, :] = q_buf[:, h * latent_width : (h + 1) * latent_width].astype(jnp.float32)
            tall_rope[own, :] = q_rope_buf[:, h * rope_width : (h + 1) * rope_width].astype(jnp.float32)
        queries, rope_queries = tall[...].astype(jnp.bfloat16), tall_rope[...].astype(jnp.bfloat16)
        request = lax.broadcasted_iota(jnp.int32, (requests, 1), 0)
        begin, end, start = jnp.zeros_like(request), jnp.zeros_like(request), jnp.int32(0)
        for r in range(requests):
            begin = jnp.where(request == r, start, begin)
            start = start + lengths_buf[0, r]
            end = jnp.where(request == r, start, end)
        position = lax.broadcasted_iota(jnp.int32, (requests, total), 1)
        bias = jnp.where((position >= begin) & (position < end), 0.0, -jnp.inf)
        highest = jnp.full((heads_here, requests, LANES), -jnp.inf, jnp.float32)
        for (k, n), copy in zip(chunks, copies[4:]):
            copy.wait()
            part_scores = lax.dot_general(
                queries, latent_buf[k : k + n, :], (((1,), (1,)), ((), ())), preferred_element_type=jnp.float32
            ) + jnp.dot(rope_queries, rope_buf[:, k : k + n], preferred_element_type=jnp.float32)
            masked = part_scores.reshape(heads_here, requests, n) + bias[None, :, k : k + n]
            scores[:, k : k + n] = masked.reshape(rows, n)
            for j in range(0, n, LANES):
                highest = jnp.maximum(highest, masked[:, :, j : j + LANES])
        scale = score_scale * LOG2E
        top = jnp.max(highest, axis=2, keepdims=True).reshape(rows, 1) * scale
        step = min(rows, 256)
        for k in range(0, rows, step):
            own = slice(k, k + step)
            weights = jnp.exp2(scores[own, :] * scale - top[own])
            whole = 1.0 / jnp.sum(weights, axis=1, keepdims=True)
            result = jnp.dot(weights.astype(jnp.bfloat16), latent_buf[...], preferred_element_type=jnp.float32) * whole
            for j in range(0, step, requests):
                h = (k + j) // requests
                out_buf[:, h * latent_width : (h + 1) * latent_width] = result[j : j + requests].astype(jnp.bfloat16)
        last = pltpu.make_async_copy(out_buf, out_ref.at[:, pl.ds(part * wide, wide)], sems.at[len(pairs)])
        last.start()
        for copy in copies[4 + len(chunks) :]:
            copy.wait()
        last.wait()

    extra = [in_hbm(weight)] if early else []
    return pl.pallas_call(
        kernel,
        out_shape=[pltpu.HBM(q_latent.shape, jnp.bfloat16)] + [pltpu.VMEM(e.shape, e.dtype) for e in early],
        in_specs=[pl.BlockSpec(memory_space=pltpu.SMEM)]
        + [pl.BlockSpec(memory_space=pl.ANY)] * (5 + len(done) + len(extra)),
        out_specs=[pl.BlockSpec(memory_space=pl.ANY)] + on_chip(len(early)),
        input_output_aliases={6: 0} if done else {},
        scratch_shapes=[
            pltpu.SMEM(lengths.shape, lengths.dtype),
            pltpu.VMEM((requests, wide), jnp.bfloat16),
            pltpu.VMEM((requests, thin), jnp.bfloat16),
            pltpu.VMEM(latent.shape, latent.dtype),
            pltpu.VMEM(rope_keys.shape, rope_keys.dtype),
            pltpu.VMEM((rows, latent_width), jnp.float32),
            pltpu.VMEM((rows, rope_width), jnp.float32),
            pltpu.VMEM((rows, total), jnp.float32),
            pltpu.VMEM((requests, wide), jnp.bfloat16),
            pltpu.SemaphoreType.DMA((5 + len(chunks) + len(early),)),
        ],
        compiler_params=pltpu.CompilerParams(vmem_limit_bytes=16 * MIB),
        cost_estimate=pl.CostEstimate(
            flops=2 * rows * total * (2 * latent_width + rope_width),
            bytes_accessed=4 * MIB,
            transcendentals=rows * total,
        ),
    )(share[None], *[in_hbm(x) for x in (lengths, q_latent, q_rope, latent, rope_keys)], *done, *extra)


def cuts(total, most):
    step = next(s for s in (512, 256, 128, 64, 32, 16) if s <= most and total % s == 0)
    return [(k, step) for k in range(0, total, step)]


def pack_kernel(tokens_ref, routes_ref, gates_ref, out_ref, tokens_buf, routes_buf, gates_buf, sems):
    width = tokens_ref.shape[1]
    copies = [
        pltpu.make_async_copy(source, target, sems.at[k])
        for k, (source, target) in enumerate(
            ((tokens_ref, tokens_buf), (routes_ref, routes_buf), (gates_ref, gates_buf))
        )
    ]
    for copy in copies:
        copy.start()
    for copy in copies[1:]:
        copy.wait()
    label = lax.broadcasted_iota(jnp.int32, (tokens_ref.shape[0], LANES), 1)
    table = jnp.zeros(label.shape, jnp.float32)
    for k in range(routes_ref.shape[1]):
        gate = gates_buf[:, k : k + 1].astype(jnp.float32)
        table += jnp.where(routes_buf[:, k : k + 1] == label, gate, 0.0)
    copies[0].wait()
    for j in range(out_ref.shape[0]):
        out_ref[j, :, :width] = tokens_buf[...]
        out_ref[j, :, width:] = table.astype(jnp.bfloat16)


def pack(tokens, routes, gates, copies):
    return pl.pallas_call(
        pack_kernel,
        out_shape=jax.ShapeDtypeStruct((copies, tokens.shape[0], tokens.shape[1] + LANES), tokens.dtype),
        in_specs=[pl.BlockSpec(memory_space=pl.ANY)] * 3,
        out_specs=pl.BlockSpec(memory_space=pltpu.VMEM),
        scratch_shapes=[
            pltpu.VMEM(tokens.shape, tokens.dtype),
            pltpu.VMEM(routes.shape, routes.dtype),
            pltpu.VMEM(gates.shape, gates.dtype),
            pltpu.SemaphoreType.DMA((3,)),
        ],
        compiler_params=pltpu.CompilerParams(vmem_limit_bytes=8 * MIB),
    )(in_hbm(tokens), in_hbm(routes), in_hbm(gates))


def experts(own_expert, share, shares, rows, w_gate, w_up, w_down, early):
    width = w_down.shape[1]
    ff = w_down.shape[0] // shares
    thin, wide = cuts(width, 512), cuts(ff, 64)

    def kernel(expert_ref, share_ref, rows_ref, gate_ref, up_ref, down_ref, *refs):
        early_refs, (out_ref, gate_buf, up_buf, down_buf, out_buf, sems) = refs[: len(early)], refs[len(early) :]
        begin = pl.multiple_of(share_ref[0] * ff, ff) if shares > 1 else 0
        copies = [[], [], []]
        for n, (source, target) in enumerate(((gate_ref, gate_buf), (up_ref, up_buf), (down_ref, down_buf))):
            for k, step in wide if n == 2 else thin[0 if n else len(early) :]:
                place = (pl.ds(begin + k, step), slice(None)) if n == 2 else (pl.ds(k, step), pl.ds(begin, ff))
                copy = pltpu.make_async_copy(
                    source.at[place], target.at[pl.ds(k, step)], sems.at[sum(map(len, copies))]
                )
                copy.start()
                copies[n].append(copy)
        count = rows_ref.shape[0] * rows_ref.shape[1]
        packed = rows_ref[...].reshape(count, rows_ref.shape[2])
        table = packed[:, width:].astype(jnp.float32)
        label = lax.broadcasted_iota(jnp.int32, table.shape, 1)
        weight = jnp.sum(jnp.where(label == expert_ref[0], table, 0.0), axis=1, keepdims=True)

        def against(left, parts, waits, buf):
            total = 0.0
            for (k, step), copy in zip(parts, waits):
                copy.wait()
                total += jnp.dot(left[:, k : k + step], buf[k : k + step, :], preferred_element_type=jnp.float32)
            return total

        gate_pre = 0.0
        for (k, step), ref in zip(thin, early_refs):
            gate_pre += jnp.dot(packed[:, k : k + step], ref[...], preferred_element_type=jnp.float32)
        gate_pre += against(packed, thin[len(early) :], copies[0], gate_buf)
        up_pre = against(packed, thin, copies[1], up_buf)
        hidden = (gate_pre / (1.0 + jnp.exp(-gate_pre)) * up_pre).astype(jnp.bfloat16)
        total = against(hidden, wide, copies[2], down_buf)
        out_buf[...] = (total * weight).astype(jnp.bfloat16).reshape(out_buf.shape)
        last = pltpu.make_async_copy(out_buf, out_ref, sems.at[sum(map(len, copies))])
        last.start()
        last.wait()

    return pl.pallas_call(
        kernel,
        out_shape=pltpu.HBM(rows.shape[:2] + (width,), jnp.bfloat16),
        in_specs=[pl.BlockSpec(memory_space=pltpu.SMEM)] * 2
        + on_chip(1)
        + [pl.BlockSpec(memory_space=pl.ANY)] * 3
        + on_chip(len(early)),
        out_specs=pl.BlockSpec(memory_space=pl.ANY),
        scratch_shapes=[
            pltpu.VMEM((width, ff), w_gate.dtype),
            pltpu.VMEM((width, ff), w_up.dtype),
            pltpu.VMEM((ff, width), w_down.dtype),
            pltpu.VMEM(rows.shape[:2] + (width,), jnp.bfloat16),
            pltpu.SemaphoreType.DMA((2 * len(thin) + len(wide) + 1,)),
        ],
        compiler_params=pltpu.CompilerParams(vmem_limit_bytes=6 * width * ff + 10 * MIB),
    )(own_expert[None], share[None], rows, in_hbm(w_gate), in_hbm(w_up), in_hbm(w_down), *early)


def local(q_latent, q_rope, cache_latent, cache_rope, lengths, tokens_b, routes, gates, w_gate, w_up, w_down):
    pool_count = lax.axis_size("pool")
    head_count = lax.axis_size("heads")
    slices = pool_count * head_count // EXPERTS
    own_expert = (lax.axis_index("pool") * head_count + lax.axis_index("heads")) // slices
    group_count = lax.axis_size("groups")
    apart = w_down.shape[0] % (group_count * 256) == 0
    shares, axes = (group_count, ("groups", "pool")) if apart else (1, ("pool",))
    peers = pool_count * shares
    middle = peers * 3 // 4
    order = [middle] + [i for i in reversed(range(peers)) if i != middle]

    def swap(blocks):
        return lax.all_to_all(blocks, axes, split_axis=0, concat_axis=0, tiled=True, axis_index_groups=[order])

    rows = swap(pack(tokens_b, routes, gates, peers))
    share = lax.axis_index("groups").astype(jnp.int32) if apart else jnp.int32(0)
    ff = w_down.shape[0] // shares
    model_width = tokens_b.shape[1]
    step = cuts(model_width, 512)[0][1]
    pieces = min(model_width // step, EARLY // (2 * step * ff))
    pieces = [jax.ShapeDtypeStruct((step, ff), w_gate.dtype)] * pieces
    inputs = (q_latent, q_rope, cache_latent, cache_rope, lengths)
    half, *early = attend(0, 2, *inputs, [], w_gate, share, pieces)
    rows, half, *early = lax.optimization_barrier((rows, half, *early))
    terms = experts(own_expert, share, shares, rows, w_gate, w_up, w_down, early)
    terms, half = lax.optimization_barrier((terms, half))
    returned = swap(terms)
    (attended,) = attend(1, 2, *inputs, [half], w_gate, share, [])
    returned, attended = lax.optimization_barrier((returned, attended))
    local_sum = jnp.sum(returned.astype(jnp.float32), axis=0)
    other = lax.ppermute(local_sum, "heads", [(0, 1), (1, 0)])
    moe_out = (local_sum + other).astype(jnp.bfloat16)
    return (attended, moe_out)


def solution(mesh):
    rows = P(("groups", "pool"), None)
    split = P(("groups", "pool"), "heads")
    placed = (split, split, rows, P(None, ("groups", "pool")), rows, rows, rows, rows)
    weights = (P(None, ("pool", "heads")),) * 2 + (P(("pool", "heads"), None),)
    return jax.shard_map(
        local, mesh=mesh, in_specs=placed + weights, out_specs=(split, rows), check_vma=False
    )
```

```python
import jax
import jax.numpy as jnp
from jax import lax
from jax.experimental import pallas as pl
from jax.experimental.pallas import tpu as pltpu
from jax.sharding import PartitionSpec as P

EXPERTS = 16
LANES = 128
MIB = 1 << 20
EARLY = 3 * MIB

score_scale = 192.0 ** (-0.5)
LOG2E = 1.4426950408889634


def on_chip(count):
    return [pl.BlockSpec(memory_space=pltpu.VMEM)] * count


def in_hbm(array):
    return pltpu.with_memory_space_constraint(array, pltpu.HBM)


def attend(part, parts, q_latent, q_rope, latent, rope_keys, lengths, done, weight, share, early):
    requests, total, latent_width = lengths.shape[1], latent.shape[0], latent.shape[1]
    rope_width = rope_keys.shape[0]
    heads_here = q_latent.shape[1] // latent_width // parts
    rows = heads_here * requests
    block = min(1024, total)
    wide, thin = heads_here * latent_width, heads_here * rope_width
    ff = early[0].shape[1] if early else 0
    chunks = [(k, block) for k in range(0, total, block)]

    def kernel(share_ref, lengths_ref, q_ref, q_rope_ref, latent_ref, rope_ref, *refs):
        rest = len(done) + (1 if early else 0)
        out_ref, piece_refs = refs[rest], refs[rest + 1 : rest + 1 + len(early)]
        (lengths_buf, q_buf, q_rope_buf, latent_buf, rope_buf, tall, tall_rope, scores, out_buf, sems) = refs[
            rest + 1 + len(early) :
        ]
        pairs = [
            (lengths_ref, lengths_buf),
            (q_ref.at[:, pl.ds(part * wide, wide)], q_buf),
            (q_rope_ref.at[:, pl.ds(part * thin, thin)], q_rope_buf),
            (rope_ref, rope_buf),
        ] + [(latent_ref.at[pl.ds(k, n)], latent_buf.at[pl.ds(k, n)]) for k, n in chunks]
        if early:
            begin = pl.multiple_of(share_ref[0] * ff, LANES)
            for k, piece_ref in enumerate(piece_refs):
                n = piece_ref.shape[0]
                pairs.append((refs[len(done)].at[pl.ds(k * n, n), pl.ds(begin, ff)], piece_ref))
        copies = [pltpu.make_async_copy(source, target, sems.at[k]) for k, (source, target) in enumerate(pairs)]
        for copy in copies:
            copy.start()
        for copy in copies[:4]:
            copy.wait()
        for h in range(heads_here):
            own = slice(h * requests, (h + 1) * requests)
            tall[own, :] = q_buf[:, h * latent_width : (h + 1) * latent_width].astype(jnp.float32)
            tall_rope[own, :] = q_rope_buf[:, h * rope_width : (h + 1) * rope_width].astype(jnp.float32)
        queries, rope_queries = tall[...].astype(jnp.bfloat16), tall_rope[...].astype(jnp.bfloat16)
        request = lax.broadcasted_iota(jnp.int32, (requests, 1), 0)
        begin, end, start = jnp.zeros_like(request), jnp.zeros_like(request), jnp.int32(0)
        for r in range(requests):
            begin = jnp.where(request == r, start, begin)
            start = start + lengths_buf[0, r]
            end = jnp.where(request == r, start, end)
        position = lax.broadcasted_iota(jnp.int32, (requests, total), 1)
        bias = jnp.where((position >= begin) & (position < end), 0.0, -jnp.inf)
        highest = jnp.full((heads_here, requests, LANES), -jnp.inf, jnp.float32)
        for (k, n), copy in zip(chunks, copies[4:]):
            copy.wait()
            part_scores = lax.dot_general(
                queries, latent_buf[k : k + n, :], (((1,), (1,)), ((), ())), preferred_element_type=jnp.float32
            ) + jnp.dot(rope_queries, rope_buf[:, k : k + n], preferred_element_type=jnp.float32)
            masked = part_scores.reshape(heads_here, requests, n) + bias[None, :, k : k + n]
            scores[:, k : k + n] = masked.reshape(rows, n)
            for j in range(0, n, LANES):
                highest = jnp.maximum(highest, masked[:, :, j : j + LANES])
        scale = score_scale * LOG2E
        top = jnp.max(highest, axis=2, keepdims=True).reshape(rows, 1) * scale
        step = min(rows, 256)
        for k in range(0, rows, step):
            own = slice(k, k + step)
            weights = jnp.exp2(scores[own, :] * scale - top[own])
            whole = 1.0 / jnp.sum(weights, axis=1, keepdims=True)
            result = jnp.dot(weights.astype(jnp.bfloat16), latent_buf[...], preferred_element_type=jnp.float32) * whole
            for j in range(0, step, requests):
                h = (k + j) // requests
                out_buf[:, h * latent_width : (h + 1) * latent_width] = result[j : j + requests].astype(jnp.bfloat16)
        last = pltpu.make_async_copy(out_buf, out_ref.at[:, pl.ds(part * wide, wide)], sems.at[len(pairs)])
        last.start()
        for copy in copies[4 + len(chunks) :]:
            copy.wait()
        last.wait()

    extra = [in_hbm(weight)] if early else []
    return pl.pallas_call(
        kernel,
        out_shape=[pltpu.HBM(q_latent.shape, jnp.bfloat16)] + [pltpu.VMEM(e.shape, e.dtype) for e in early],
        in_specs=[pl.BlockSpec(memory_space=pltpu.SMEM)]
        + [pl.BlockSpec(memory_space=pl.ANY)] * (5 + len(done) + len(extra)),
        out_specs=[pl.BlockSpec(memory_space=pl.ANY)] + on_chip(len(early)),
        input_output_aliases={6: 0} if done else {},
        scratch_shapes=[
            pltpu.SMEM(lengths.shape, lengths.dtype),
            pltpu.VMEM((requests, wide), jnp.bfloat16),
            pltpu.VMEM((requests, thin), jnp.bfloat16),
            pltpu.VMEM(latent.shape, latent.dtype),
            pltpu.VMEM(rope_keys.shape, rope_keys.dtype),
            pltpu.VMEM((rows, latent_width), jnp.float32),
            pltpu.VMEM((rows, rope_width), jnp.float32),
            pltpu.VMEM((rows, total), jnp.float32),
            pltpu.VMEM((requests, wide), jnp.bfloat16),
            pltpu.SemaphoreType.DMA((5 + len(chunks) + len(early),)),
        ],
        compiler_params=pltpu.CompilerParams(vmem_limit_bytes=16 * MIB),
        cost_estimate=pl.CostEstimate(
            flops=2 * rows * total * (2 * latent_width + rope_width),
            bytes_accessed=4 * MIB,
            transcendentals=rows * total,
        ),
    )(share[None], *[in_hbm(x) for x in (lengths, q_latent, q_rope, latent, rope_keys)], *done, *extra)


def cuts(total, most):
    step = next(s for s in (512, 256, 128, 64, 32, 16) if s <= most and total % s == 0)
    return [(k, step) for k in range(0, total, step)]


def pack_kernel(tokens_ref, routes_ref, gates_ref, out_ref, tokens_buf, routes_buf, gates_buf, sems):
    width = tokens_ref.shape[1]
    copies = [
        pltpu.make_async_copy(source, target, sems.at[k])
        for k, (source, target) in enumerate(
            ((tokens_ref, tokens_buf), (routes_ref, routes_buf), (gates_ref, gates_buf))
        )
    ]
    for copy in copies:
        copy.start()
    for copy in copies[1:]:
        copy.wait()
    label = lax.broadcasted_iota(jnp.int32, (tokens_ref.shape[0], LANES), 1)
    table = jnp.zeros(label.shape, jnp.float32)
    for k in range(routes_ref.shape[1]):
        gate = gates_buf[:, k : k + 1].astype(jnp.float32)
        table += jnp.where(routes_buf[:, k : k + 1] == label, gate, 0.0)
    copies[0].wait()
    for j in range(out_ref.shape[0]):
        out_ref[j, :, :width] = tokens_buf[...]
        out_ref[j, :, width:] = table.astype(jnp.bfloat16)


def pack(tokens, routes, gates, copies):
    return pl.pallas_call(
        pack_kernel,
        out_shape=jax.ShapeDtypeStruct((copies, tokens.shape[0], tokens.shape[1] + LANES), tokens.dtype),
        in_specs=[pl.BlockSpec(memory_space=pl.ANY)] * 3,
        out_specs=pl.BlockSpec(memory_space=pltpu.VMEM),
        scratch_shapes=[
            pltpu.VMEM(tokens.shape, tokens.dtype),
            pltpu.VMEM(routes.shape, routes.dtype),
            pltpu.VMEM(gates.shape, gates.dtype),
            pltpu.SemaphoreType.DMA((3,)),
        ],
        compiler_params=pltpu.CompilerParams(vmem_limit_bytes=8 * MIB),
    )(in_hbm(tokens), in_hbm(routes), in_hbm(gates))


def experts(own_expert, share, shares, rows, w_gate, w_up, w_down, early):
    width = w_down.shape[1]
    ff = w_down.shape[0] // shares
    thin, wide = cuts(width, 512), cuts(ff, 64)

    def kernel(expert_ref, share_ref, rows_ref, gate_ref, up_ref, down_ref, *refs):
        early_refs, (out_ref, gate_buf, up_buf, down_buf, out_buf, sems) = refs[: len(early)], refs[len(early) :]
        begin = pl.multiple_of(share_ref[0] * ff, ff) if shares > 1 else 0
        copies = [[], [], []]
        for n, (source, target) in enumerate(((gate_ref, gate_buf), (up_ref, up_buf), (down_ref, down_buf))):
            for k, step in wide if n == 2 else thin[0 if n else len(early) :]:
                place = (pl.ds(begin + k, step), slice(None)) if n == 2 else (pl.ds(k, step), pl.ds(begin, ff))
                copy = pltpu.make_async_copy(
                    source.at[place], target.at[pl.ds(k, step)], sems.at[sum(map(len, copies))]
                )
                copy.start()
                copies[n].append(copy)
        count = rows_ref.shape[0] * rows_ref.shape[1]
        packed = rows_ref[...].reshape(count, rows_ref.shape[2])
        table = packed[:, width:].astype(jnp.float32)
        label = lax.broadcasted_iota(jnp.int32, table.shape, 1)
        weight = jnp.sum(jnp.where(label == expert_ref[0], table, 0.0), axis=1, keepdims=True)

        def against(left, parts, waits, buf):
            total = 0.0
            for (k, step), copy in zip(parts, waits):
                copy.wait()
                total += jnp.dot(left[:, k : k + step], buf[k : k + step, :], preferred_element_type=jnp.float32)
            return total

        gate_pre = 0.0
        for (k, step), ref in zip(thin, early_refs):
            gate_pre += jnp.dot(packed[:, k : k + step], ref[...], preferred_element_type=jnp.float32)
        gate_pre += against(packed, thin[len(early) :], copies[0], gate_buf)
        up_pre = against(packed, thin, copies[1], up_buf)
        hidden = (gate_pre / (1.0 + jnp.exp(-gate_pre)) * up_pre).astype(jnp.bfloat16)
        total = against(hidden, wide, copies[2], down_buf)
        out_buf[...] = (total * weight).astype(jnp.bfloat16).reshape(out_buf.shape)
        last = pltpu.make_async_copy(out_buf, out_ref, sems.at[sum(map(len, copies))])
        last.start()
        last.wait()

    return pl.pallas_call(
        kernel,
        out_shape=pltpu.HBM(rows.shape[:2] + (width,), jnp.bfloat16),
        in_specs=[pl.BlockSpec(memory_space=pltpu.SMEM)] * 2
        + on_chip(1)
        + [pl.BlockSpec(memory_space=pl.ANY)] * 3
        + on_chip(len(early)),
        out_specs=pl.BlockSpec(memory_space=pl.ANY),
        scratch_shapes=[
            pltpu.VMEM((width, ff), w_gate.dtype),
            pltpu.VMEM((width, ff), w_up.dtype),
            pltpu.VMEM((ff, width), w_down.dtype),
            pltpu.VMEM(rows.shape[:2] + (width,), jnp.bfloat16),
            pltpu.SemaphoreType.DMA((2 * len(thin) + len(wide) + 1,)),
        ],
        compiler_params=pltpu.CompilerParams(vmem_limit_bytes=6 * width * ff + 10 * MIB),
    )(own_expert[None], share[None], rows, in_hbm(w_gate), in_hbm(w_up), in_hbm(w_down), *early)


def local(q_latent, q_rope, cache_latent, cache_rope, lengths, tokens_b, routes, gates, w_gate, w_up, w_down):
    pool_count = lax.axis_size("pool")
    head_count = lax.axis_size("heads")
    slices = pool_count * head_count // EXPERTS
    own_expert = (lax.axis_index("pool") * head_count + lax.axis_index("heads")) // slices
    group_count = lax.axis_size("groups")
    apart = w_down.shape[0] % (group_count * 256) == 0
    shares, axes = (group_count, ("groups", "pool")) if apart else (1, ("pool",))
    peers = pool_count * shares
    middle = peers * 3 // 4
    order = [(middle + (peers // 2 + 1) * i) % peers for i in range(peers)]
    if len(set(order)) < peers:
        order = list(range(peers))

    def swap(blocks):
        return lax.all_to_all(blocks, axes, split_axis=0, concat_axis=0, tiled=True, axis_index_groups=[order])

    rows = swap(pack(tokens_b, routes, gates, peers))
    share = lax.axis_index("groups").astype(jnp.int32) if apart else jnp.int32(0)
    ff = w_down.shape[0] // shares
    model_width = tokens_b.shape[1]
    step = cuts(model_width, 512)[0][1]
    pieces = min(model_width // step, EARLY // (2 * step * ff))
    pieces = [jax.ShapeDtypeStruct((step, ff), w_gate.dtype)] * pieces
    inputs = (q_latent, q_rope, cache_latent, cache_rope, lengths)
    half, *early = attend(0, 2, *inputs, [], w_gate, share, pieces)
    rows, half, *early = lax.optimization_barrier((rows, half, *early))
    terms = experts(own_expert, share, shares, rows, w_gate, w_up, w_down, early)
    terms, half = lax.optimization_barrier((terms, half))
    returned = swap(terms)
    (attended,) = attend(1, 2, *inputs, [half], w_gate, share, [])
    returned, attended = lax.optimization_barrier((returned, attended))
    local_sum = jnp.sum(returned.astype(jnp.float32), axis=0)
    other = lax.ppermute(local_sum, "heads", [(0, 1), (1, 0)])
    moe_out = (local_sum + other).astype(jnp.bfloat16)
    return (attended, moe_out)


def solution(mesh):
    rows = P(("groups", "pool"), None)
    split = P(("groups", "pool"), "heads")
    placed = (split, split, rows, P(None, ("groups", "pool")), rows, rows, rows, rows)
    weights = (P(None, ("pool", "heads")),) * 2 + (P(("pool", "heads"), None),)
    return jax.shard_map(
        local, mesh=mesh, in_specs=placed + weights, out_specs=(split, rows), check_vma=False
    )
```
